32 devices in a mesh: grp: 8 (over z, x), mem: 4 (over y, core).
Axes of the slice: x: 2, y: 2, z: 4, core: 2. Of those that a mesh axis runs over, the one named last changes fastest.
Arguments:
- state: float32 [3, 128, 16, 128], P(None, ('grp', 'mem')), may hold values from -0.18 to 0.18
- direction: float32 [3, 128, 16, 128], P(None, ('grp', 'mem')), may hold values from -0.6 to 0.6
- rhs: float32 [3, 128, 16, 128], P(None, ('grp', 'mem')), may hold values from -6 to 6
- clamp: int32 [128, 16], P(('grp', 'mem')), may hold values 0 or 1
- stiffness: float32 [32, 4, 32], P(('grp', 'mem')), may hold values from 0.5 to 5
- coarse_owner: int32 [32, 128], P(('grp', 'mem')), may hold values from 0 to 127, as said below
- coarse_inverse: float32 [32, 2, 192, 192], P(('grp', 'mem')), may hold values from -0.006 to 0.006
Outputs:
- new_direction: float32 [3, 128, 16, 128], P(None, ('grp', 'mem'))
- residual: float32 [3, 128, 16, 128], P(None, ('grp', 'mem'))
- coarse_residual: float32 [3, 32, 4, 32], P(None, ('grp', 'mem'))
The draws below stay inside these ranges and needn't reach their ends.
Inputs may be any that keep to these rules, and one draw needn't show every extreme that they name: `coarse_owner`: each layer's row is a permutation of 0 to 127.
All inputs are finite; a program needn't handle non-finite values. No bound on the sum of `clamp` on one device may be relied on, other than what follows from the above.
Results may differ from the reference program's by a relative error of at most 0.0003.
Values sent between devices are 32-bit elements; how exact they have to be, the bound alone decides.
A program may use at most 64 MiB of HBM per device.

```python
import math
import jax
import jax.numpy as jnp
import numpy as np
from jax import lax

EY = 4
EZ = 32
VB = 64
LAYERS = 32
NBLK = 2
N_GRP = 8


def draw_coarse_owner(key, part):
    row_keys = jax.random.split(key, LAYERS)
    return jax.vmap(lambda k: jax.random.permutation(k, EY * EZ))(row_keys).astype(jnp.int32)


def set_ends(values, rng, low, high):
    shape = values.shape
    index_at = [jax.random.randint(jax.random.fold_in(rng, axis), (), 0, shape[axis]) for axis in range(len(shape))]
    values = values.at[tuple(index_at)].set(low)
    longest = shape.index(max(shape))
    index_at[longest] = (index_at[longest] + 1) % shape[longest]
    return values.at[tuple(index_at)].set(high)


def shard_levels(stream_key, extent, shards, smallest, high):
    level = 1.0
    for position, shards_of in shards:
        steps = jax.random.uniform(jax.random.fold_in(jax.random.fold_in(stream_key, 6), position), (shards_of,), jnp.float32, smallest / len(shards), high / len(shards))
        level = level * jnp.repeat(jnp.exp(steps), extent[position] // shards_of).reshape((-1,) + (1,) * (len(extent) - 1 - position))
    return level


def centred(rng, extent, scale, reach, cuts=(), kind=jnp.bfloat16):
    values = jax.random.normal(rng, extent, jnp.float32) * scale
    if len(cuts) > 0:
        values = shard_levels(rng, extent, cuts, -0.22, 0.18) * values
    return jnp.clip(values, min=-reach, max=reach).astype(kind)


def setup_inputs(seed: int = 0) -> dict:
    seeds = jax.random.split(jax.random.key(seed), 8)
    state = centred(seeds[0], (3, 4 * LAYERS, 4 * EY, 4 * EZ), 0.03, 0.18, ((1, 32),), jnp.float32)
    direction = centred(seeds[1], (3, 4 * LAYERS, 4 * EY, 4 * EZ), 0.1, 0.6, ((1, 32),), jnp.float32)
    rhs = centred(seeds[2], (3, 4 * LAYERS, 4 * EY, 4 * EZ), 1.0, 6.0, ((1, 32),), jnp.float32)
    clamp = set_ends((jax.random.randint(seeds[3], (4 * LAYERS, 4 * EY), 0, 4) < 1).astype(jnp.int32), jax.random.fold_in(seeds[3], 1), 0, 1)
    stiffness = jnp.clip(jnp.exp(math.log(5.0) - 2.3025851 * jax.random.uniform(seeds[4], (LAYERS, EY, EZ), jnp.float32) ** shard_levels(seeds[4], (LAYERS, EY, EZ), ((0, 32),), -0.2, 0.2)), 0.5, 5.0)
    coarse_owner = draw_coarse_owner(jax.random.fold_in(seeds[7], 71), 0)
    coarse_inverse = centred(seeds[6], (LAYERS, NBLK, 3 * VB, 3 * VB), 0.001, 0.006, ((0, 32),), jnp.float32)
    return {"state": state, "direction": direction, "rhs": rhs, "clamp": clamp, "stiffness": stiffness, "coarse_owner": coarse_owner, "coarse_inverse": coarse_inverse}


LAME_FIRST = 1.2
LAME_SHEAR = 0.8
HIGHEST = lax.Precision.HIGHEST

def gauss_rule():
    inner = np.sqrt(5.0 - 2.0 * np.sqrt(10.0 / 7.0)) / 3.0
    outer = np.sqrt(5.0 + 2.0 * np.sqrt(10.0 / 7.0)) / 3.0
    inner_weight = (322.0 + 13.0 * np.sqrt(70.0)) / 900.0
    outer_weight = (322.0 - 13.0 * np.sqrt(70.0)) / 900.0
    points = np.array([-outer, -inner, 0.0, inner, outer])
    weights = np.array([outer_weight, inner_weight, 128.0 / 225.0, inner_weight, outer_weight])
    return (points, weights)

def basis_tables():
    gll_points = np.array([-1.0, -np.sqrt(3.0 / 7.0), 0.0, np.sqrt(3.0 / 7.0), 1.0])
    gauss_points, gauss_weights = gauss_rule()
    values = np.zeros((5, 5))
    slopes = np.zeros((5, 5))
    for j in range(5):
        others = [gll_points[k] for k in range(5) if k != j]
        denominator = np.prod([gll_points[j] - o for o in others])
        for q in range(5):
            t = gauss_points[q]
            values[q, j] = np.prod([t - o for o in others]) / denominator
            total = 0.0
            for i in range(4):
                total += np.prod([t - others[k] for k in range(4) if k != i])
            slopes[q, j] = 2.0 * total / denominator
    return (gll_points, gauss_weights, values, slopes)

def banded(table, count):
    banded_matrix = np.zeros((5 * count, 4 * count + 1))
    for e in range(count):
        banded_matrix[5 * e:5 * e + 5, 4 * e:4 * e + 5] = table
    return banded_matrix

def restrictor(gll_points, count):
    result = np.zeros((count, 4 * count))
    for e in range(count):
        for j in range(4):
            result[e, 4 * e + j] += (1.0 - gll_points[j]) / 2.0
            if e + 1 < count:
                result[e + 1, 4 * e + j] += (1.0 + gll_points[j]) / 2.0
    return result

def operators(count_y, count_z):
    gll_points, gauss_weights, values, slopes = basis_tables()
    return (jnp.asarray(values, jnp.float32), jnp.asarray(slopes, jnp.float32), jnp.asarray(banded(values, count_y), jnp.float32), jnp.asarray(banded(slopes, count_y), jnp.float32), jnp.asarray(banded(values, count_z), jnp.float32), jnp.asarray(banded(slopes, count_z), jnp.float32))

def gradient(field, mats, low, high):
    basis_x, slope_x, basis_y, slope_y, basis_z, slope_z = mats
    basis_x = basis_x[:, low:high]
    slope_x = slope_x[:, low:high]
    along_b = jnp.einsum('cxyz,qz->cxyq', field, basis_z, precision=HIGHEST)
    along_d = jnp.einsum('cxyz,qz->cxyq', field, slope_z, precision=HIGHEST)
    plain_b = jnp.einsum('cxyq,py->cxpq', along_b, basis_y, precision=HIGHEST)
    sloped_b = jnp.einsum('cxyq,py->cxpq', along_b, slope_y, precision=HIGHEST)
    plain_d = jnp.einsum('cxyq,py->cxpq', along_d, basis_y, precision=HIGHEST)
    grad_x = jnp.einsum('cxpq,rx->crpq', plain_b, slope_x, precision=HIGHEST)
    grad_y = jnp.einsum('cxpq,rx->crpq', sloped_b, basis_x, precision=HIGHEST)
    grad_z = jnp.einsum('cxpq,rx->crpq', plain_d, basis_x, precision=HIGHEST)
    return (grad_x, grad_y, grad_z)

def divergence(fluxes, mats):
    basis_x, slope_x, basis_y, slope_y, basis_z, slope_z = mats
    part_x = jnp.einsum('crpq,rx->cxpq', fluxes[0], slope_x, precision=HIGHEST)
    part_y = jnp.einsum('crpq,rx->cxpq', fluxes[1], basis_x, precision=HIGHEST)
    part_z = jnp.einsum('crpq,rx->cxpq', fluxes[2], basis_x, precision=HIGHEST)
    side_b = jnp.einsum('cxpq,py->cxyq', part_x, basis_y, precision=HIGHEST) + jnp.einsum('cxpq,py->cxyq', part_y, slope_y, precision=HIGHEST)
    side_d = jnp.einsum('cxpq,py->cxyq', part_z, basis_y, precision=HIGHEST)
    return jnp.einsum('cxyq,qz->cxyz', side_b, basis_z, precision=HIGHEST) + jnp.einsum('cxyq,qz->cxyz', side_d, slope_z, precision=HIGHEST)

def state_terms(gradients):
    deform = [[gradients[a][c] + (1.0 if c == a else 0.0) for a in range(3)] for c in range(3)]
    strain = [[0.5 * (deform[0][a] * deform[0][b] + deform[1][a] * deform[1][b] + deform[2][a] * deform[2][b]) - (0.5 if a == b else 0.0) for b in range(3)] for a in range(3)]
    strain_trace = strain[0][0] + strain[1][1] + strain[2][2]
    stress = [[2.0 * LAME_SHEAR * strain[a][b] + (LAME_FIRST * strain_trace if a == b else 0.0) for b in range(3)] for a in range(3)]
    return (deform, stress)

def tangent_flux(gradients, deform, stress, weighting):
    change = [[gradients[a][c] for a in range(3)] for c in range(3)]
    cross_terms = [[deform[0][a] * change[0][b] + deform[1][a] * change[1][b] + deform[2][a] * change[2][b] for b in range(3)] for a in range(3)]
    strain_change = [[0.5 * (cross_terms[a][b] + cross_terms[b][a]) for b in range(3)] for a in range(3)]
    trace_change = strain_change[0][0] + strain_change[1][1] + strain_change[2][2]
    stress_change = [[2.0 * LAME_SHEAR * strain_change[a][b] + (LAME_FIRST * trace_change if a == b else 0.0) for b in range(3)] for a in range(3)]
    fluxes = []
    for a in range(3):
        rows_of = []
        for c in range(3):
            entry = change[c][0] * stress[0][a] + change[c][1] * stress[1][a] + change[c][2] * stress[2][a] + deform[c][0] * stress_change[0][a] + deform[c][1] * stress_change[1][a] + deform[c][2] * stress_change[2][a]
            rows_of.append(entry * weighting)
        fluxes.append(jnp.stack(rows_of))
    return fluxes

def quad_weighting(element_stiffness, gauss_weights):
    count_y, count_z = element_stiffness.shape
    spread = jnp.repeat(jnp.repeat(element_stiffness, 5, axis=0), 5, axis=1)
    weight_y = np.tile(gauss_weights, count_y)
    weight_z = np.tile(gauss_weights, count_z)
    quadrature = gauss_weights[:, None, None] * weight_y[None, :, None] * weight_z[None, None, :] / 8.0
    return spread[None] * jnp.asarray(quadrature, jnp.float32)

def reference(state, direction, rhs, clamp, stiffness, coarse_owner, coarse_inverse):
    layers, count_y, count_z = stiffness.shape
    mats = operators(count_y, count_z)
    gll_points, gauss_weights, values, slopes = basis_tables()
    low_hat = jnp.asarray((1.0 - gll_points[:4]) / 2.0, jnp.float32)
    high_hat = jnp.asarray((1.0 + gll_points[:4]) / 2.0, jnp.float32)
    hat_y = jnp.asarray(restrictor(gll_points, count_y), jnp.float32)
    hat_z = jnp.asarray(restrictor(gll_points, count_z), jnp.float32)
    bottom = (jnp.arange(4 * count_z) == 0).astype(jnp.float32)
    keep = 1.0 - clamp.astype(jnp.float32)[:, :, None] * bottom[None, None, :]
    padded_state = jnp.pad(state, ((0, 0), (0, 1), (0, 1), (0, 1)))

    def apply_all(field):
        padded_field = jnp.pad(keep * field, ((0, 0), (0, 1), (0, 1), (0, 1)))

        def one_layer(e):
            start = (4 * e).astype(jnp.int32)
            piece = lax.dynamic_slice_in_dim(padded_field, start, 5, 1)
            state_piece = lax.dynamic_slice_in_dim(padded_state, start, 5, 1)
            element_stiffness = lax.dynamic_index_in_dim(stiffness, e, 0, keepdims=False)
            terms = state_terms(gradient(state_piece, mats, 0, 5))
            fluxes = tangent_flux(gradient(piece, mats, 0, 5), terms[0], terms[1], quad_weighting(element_stiffness, gauss_weights))
            return divergence(fluxes, mats)[:, :, :-1, :-1]
        images = lax.map(one_layer, jnp.arange(layers, dtype=jnp.int32))
        carried = jnp.concatenate([jnp.zeros_like(images[:1, :, 4]), images[:-1, :, 4]], axis=0)
        own_part = images[:, :, :4].at[:, :, 0].add(carried)
        return own_part.transpose(1, 0, 2, 3, 4).reshape(3, 4 * layers, 4 * count_y, 4 * count_z)

    def restrict(field):
        grouped = field.reshape(3, layers, 4, 4 * count_y, 4 * count_z)
        coarse_terms = jnp.einsum('cejyz,vy,wz->cejvw', grouped, hat_y, hat_z, precision=HIGHEST)
        own_part = jnp.einsum('cejvw,j->cevw', coarse_terms, low_hat, precision=HIGHEST)
        onward = jnp.einsum('cejvw,j->cevw', coarse_terms, high_hat, precision=HIGHEST)
        return own_part + jnp.concatenate([jnp.zeros_like(onward[:, :1]), onward[:, :-1]], axis=1)
    image = apply_all(direction)
    first = rhs - keep * image - (1.0 - keep) * direction
    restricted = restrict(first)
    members = layers // N_GRP
    message = count_y * count_z // N_GRP
    per_layer = restricted.transpose(1, 0, 2, 3).reshape(layers, 3, count_y * count_z)
    outgoing = jax.vmap(lambda row, slots: jnp.zeros_like(row).at[:, slots].set(row))(per_layer, coarse_owner)
    gathered = outgoing.reshape(N_GRP, members, 3, N_GRP, message).transpose(3, 1, 2, 0, 4)
    gathered = gathered.reshape(layers, 3, count_y * count_z)
    blocks = coarse_inverse.shape[1]
    block_size = coarse_inverse.shape[2] // 3
    stacked = gathered.reshape(layers, 3, blocks, block_size).transpose(0, 2, 1, 3)
    stacked = stacked.reshape(layers, blocks, 3 * block_size)
    solved = jnp.einsum('lkij,lkj->lki', coarse_inverse, stacked, precision=HIGHEST)
    solved = solved.reshape(layers, blocks, 3, block_size).transpose(0, 2, 1, 3)
    solved = solved.reshape(layers, 3, count_y * count_z)
    returned = solved.reshape(N_GRP, members, 3, N_GRP, message).transpose(3, 1, 2, 0, 4)
    returned = returned.reshape(layers, 3, count_y * count_z)
    correction = jax.vmap(lambda row, slots: row[:, slots])(returned, coarse_owner)
    correction = correction.reshape(layers, 3, count_y, count_z)
    spread_own = jnp.einsum('lcvw,vy,wz->lcyz', correction, hat_y, hat_z, precision=HIGHEST)
    spread_right = jnp.concatenate([spread_own[1:], jnp.zeros_like(spread_own[:1])], axis=0)
    prolonged = low_hat[None, None, :, None, None] * spread_own[:, :, None] + high_hat[None, None, :, None, None] * spread_right[:, :, None]
    update = keep * prolonged.transpose(1, 0, 2, 3, 4).reshape(3, 4 * layers, 4 * count_y, 4 * count_z)
    new_direction = direction + update
    image_next = apply_all(new_direction)
    residual = rhs - keep * image_next - (1.0 - keep) * new_direction
    coarse_residual = restrict(residual)
    return (new_direction, residual, coarse_residual)
```

```python
import functools

import jax
import jax.numpy as jnp
import ml_dtypes
import numpy as np
from jax import lax
from jax.experimental import pallas as pl
from jax.experimental.pallas import tpu as pltpu
from jax.sharding import PartitionSpec as P

LAME_FIRST = 1.2
LAME_SHEAR = 0.8
HIGHEST = lax.Precision.HIGHEST
MESH = pl.DeviceIdType.MESH
F32 = jnp.float32
BF16 = jnp.bfloat16
NQ = 112


def gauss_rule():
    inner = np.sqrt(5.0 - 2.0 * np.sqrt(10.0 / 7.0)) / 3.0
    outer = np.sqrt(5.0 + 2.0 * np.sqrt(10.0 / 7.0)) / 3.0
    inner_weight = (322.0 + 13.0 * np.sqrt(70.0)) / 900.0
    outer_weight = (322.0 - 13.0 * np.sqrt(70.0)) / 900.0
    points = np.array([-outer, -inner, 0.0, inner, outer])
    weights = np.array([outer_weight, inner_weight, 128.0 / 225.0, inner_weight, outer_weight])
    return (points, weights)


def basis_tables():
    gll_points = np.array([-1.0, -np.sqrt(3.0 / 7.0), 0.0, np.sqrt(3.0 / 7.0), 1.0])
    gauss_points, gauss_weights = gauss_rule()
    values = np.zeros((5, 5))
    slopes = np.zeros((5, 5))
    for j in range(5):
        others = [gll_points[k] for k in range(5) if k != j]
        denominator = np.prod([gll_points[j] - o for o in others])
        for q in range(5):
            t = gauss_points[q]
            values[q, j] = np.prod([t - o for o in others]) / denominator
            total = 0.0
            for i in range(4):
                total += np.prod([t - others[k] for k in range(4) if k != i])
            slopes[q, j] = 2.0 * total / denominator
    return (gll_points, gauss_weights, values, slopes)


def banded(table, count):
    banded_matrix = np.zeros((5 * count, 4 * count + 1))
    for e in range(count):
        banded_matrix[5 * e : 5 * e + 5, 4 * e : 4 * e + 5] = table
    return banded_matrix[:, :-1]


def restrictor(gll_points, count):
    result = np.zeros((count, 4 * count))
    for e in range(count):
        for j in range(4):
            result[e, 4 * e + j] += (1.0 - gll_points[j]) / 2.0
            if e + 1 < count:
                result[e + 1, 4 * e + j] += (1.0 + gll_points[j]) / 2.0
    return result


def halves(table):
    high = table.astype(ml_dtypes.bfloat16)
    low = (table - high.astype(np.float64)).astype(ml_dtypes.bfloat16)
    return high, low


def padded(table, axis, multiple):
    widths = [(0, 0), (0, 0)]
    widths[axis] = (0, -table.shape[axis] % multiple)
    return np.pad(table, widths)


def left_table(table):
    high, low = halves(table)
    return padded(np.concatenate([high, high, low], axis=1), 1, 128)


def right_table(table):
    high, low = halves(table)
    return np.concatenate([high, high, low], axis=0)


def constant_tables(count_y, count_z):
    gll_points, weights, values, slopes = basis_tables()
    by, dy = banded(values, count_y), banded(slopes, count_y)
    bz, dz = banded(values, count_z), banded(slopes, count_z)
    pads = lambda t: np.pad(t, ((0, NQ - t.shape[0]), (0, 0)))
    cross = np.concatenate(
        [pads(np.kron(slopes, by)), pads(np.kron(values, dy)), pads(np.kron(values, by))]
    )
    bz, dz = padded(bz, 0, 256), padded(dz, 0, 256)
    low_hat = np.append((1.0 - gll_points[:4]) / 2.0, 0.0)
    high_hat = np.append((1.0 + gll_points[:4]) / 2.0, 1.0)
    hat_y = restrictor(gll_points, count_y)
    hat_z = restrictor(gll_points, count_z)
    hats = np.zeros((16, 20 * count_y))
    hats[:count_y] = np.kron(low_hat[None], hat_y)
    hats[8 : 8 + count_y] = np.kron(high_hat[None], hat_y)
    tiled = np.tile(hat_z, (count_y, 1))
    spread_y = np.zeros((NQ, count_y))
    spread_y[:100] = np.kron(weights[:, None], np.kron(np.eye(count_y), weights[:, None])) / 8.0
    spread_z = padded(np.kron(np.eye(count_z), weights[None]), 1, 256)
    return (
        left_table(cross),
        right_table(bz.T),
        right_table(dz.T),
        np.concatenate(halves(bz), axis=1),
        np.concatenate(halves(dz), axis=1),
        left_table(cross.T),
        left_table(hats),
        right_table(tiled.T),
        right_table(tiled),
        left_table(hats.T),
        spread_y.astype(np.float32),
        spread_z.astype(np.float32),
    )


def split(x):
    high = x.astype(BF16)
    return high, (x - high.astype(F32)).astype(BF16)


def dot(a, b):
    return lax.dot_general(a, b, (((1,), (0,)), ((), ())), preferred_element_type=F32)


def dot_nt(a, b):
    return lax.dot_general(a, b, (((1,), (1,)), ((), ())), preferred_element_type=F32)


def times_right(x, table):
    high, low = split(x)
    return dot(jnp.concatenate([high, low, high], axis=1), table)


def times_left(table, x):
    high, low = split(x)
    parts = [high, low, high]
    rest = table.shape[1] - 3 * x.shape[0]
    if rest:
        parts.append(jnp.zeros((rest, x.shape[1]), BF16))
    return dot(table, jnp.concatenate(parts, axis=0))


def stacked_exact(x, one_hot, product):
    rows = x.shape[0]
    high, low = split(x)
    both = product(jnp.concatenate([high, low], axis=0), one_hot)
    return both[:rows] + both[rows:]


def iota(shape, axis):
    return lax.broadcasted_iota(jnp.int32, shape, axis)


def each(low, high, act):
    if high - low <= 8:
        for i in range(low, high):
            act(i)
    else:

        def step(i, carry):
            act(i)
            return carry

        lax.fori_loop(low, high, step, 0)


def kernel(
    groups,
    members,
    state_ref,
    direction_ref,
    rhs_ref,
    clamp_ref,
    stiff_ref,
    owner_ref,
    inverse_ref,
    cross_ref,
    bz_ref,
    dz_ref,
    bzt_ref,
    dzt_ref,
    crosst_ref,
    hats_ref,
    hatz_ref,
    hatzp_ref,
    hatst_ref,
    spready_ref,
    spreadz_ref,
    new_ref,
    residual_ref,
    coarse_ref,
    halo_tx,
    halo_state,
    halo_rx,
    sums_tx,
    sums_rx,
    solved_tx,
    solved_rx,
    last_tx,
    last_rx,
    inv_high,
    inv_low,
    weight,
    gsb,
    gsz,
    gvb,
    gvz,
    deform_s,
    stress_s,
    fbh,
    fbl,
    fzh,
    fzl,
    halo_send,
    halo_recv,
    sums_send,
    sums_recv,
    solved_send,
    solved_recv,
    last_send,
    last_recv,
):
    count_y, count_z = stiff_ref.shape[1:]
    ny = 4 * count_y
    vertices = count_y * count_z
    blocks = inverse_ref.shape[1]
    size = inverse_ref.shape[2]
    block = size // 3
    message = vertices // groups
    per_block = groups // blocks
    g = lax.axis_index("grp")
    m = lax.axis_index("mem")
    m_right = lax.rem(m + 1, members)
    m_left = lax.rem(m + members - 1, members)
    at_end = m == members - 1
    at_start = m == 0
    g_right = lax.rem(g + at_end.astype(jnp.int32), groups)
    g_left = lax.rem(g + groups - at_start.astype(jnp.int32), groups)
    is_last = (g * members + m) == groups * members - 1
    is_first = (g * members + m) == 0

    barrier = pltpu.get_barrier_semaphore()

    def greet(p, member):
        pl.semaphore_signal(barrier, inc=1, device_id=(p, member), device_id_type=MESH)

    sums_rx[...] = jnp.zeros_like(sums_rx)
    greet(g_left, m_left)
    each(1, groups, lambda d: greet(lax.rem(g_left + d, groups), m_left))
    each(0, groups, lambda d: greet(lax.rem(g_right + d, groups), m_right))
    each(1, groups, lambda d: greet(lax.rem(g + d, groups), m))

    eye = iota((ny, ny), 0) == iota((ny, ny), 1)
    clamp_rows = []
    for x in range(4):
        row = jnp.broadcast_to(clamp_ref[x : x + 1, :].astype(F32), (ny, ny))
        clamp_rows.append(jnp.sum(jnp.where(eye, row, 0.0), axis=1, keepdims=True))
    clamped = jnp.concatenate(clamp_rows, axis=0)
    lanes = 4 * count_z
    keep = jnp.where(iota((4 * ny, lanes), 1) == 0, 1.0 - clamped, 1.0)
    for c in range(3):
        halo_tx[c * ny : (c + 1) * ny, :] = keep[:ny] * direction_ref[c, 0]
    halo_tx[3 * ny : 4 * ny, :] = keep[:ny]
    halo_tx[4 * ny : 4 * ny + 8, :] = jnp.broadcast_to(owner_ref[...].astype(F32), (8, vertices))
    pl.semaphore_wait(barrier, 3 * groups - 1)

    left = (g_left, m_left)
    right = (g_right, m_right)

    def remote(src, dst, send, recv, device):
        return pltpu.make_async_remote_copy(
            src_ref=src, dst_ref=dst, send_sem=send, recv_sem=recv, device_id=device, device_id_type=MESH
        )

    copy_state = remote(state_ref.at[:, 0], halo_state, halo_send.at[0], halo_recv.at[0], left)
    copy_state.start()
    copy_halo = remote(halo_tx, halo_rx, halo_send.at[1], halo_recv.at[1], left)
    copy_halo.start()

    inv_high[...] = jnp.zeros_like(inv_high)
    inv_low[...] = jnp.zeros_like(inv_low)
    for b in range(blocks):
        high, low = split(inverse_ref[0, b])
        inv_high[b, :size, :size] = high
        inv_low[b, :size, :size] = low
    along_y = jnp.zeros((NQ, count_z), F32)
    for k in range(count_y):
        along_y = along_y + spready_ref[:, k : k + 1] * stiff_ref[0, k : k + 1, :]
    weight[...] = jnp.dot(along_y, spreadz_ref[...], precision=HIGHEST, preferred_element_type=F32)
    own_hot = (owner_ref[...] == iota((vertices, vertices), 0)).astype(F32).astype(BF16)

    def gradients(field, to_b, to_z):
        parts = times_left(cross_ref[...], field)
        plain = jnp.concatenate([parts[: 2 * NQ, c * lanes : (c + 1) * lanes] for c in range(3)], axis=0)
        sloped = jnp.concatenate([parts[2 * NQ :, c * lanes : (c + 1) * lanes] for c in range(3)], axis=0)
        to_b[...] = times_right(plain, bz_ref[...])
        to_z[...] = times_right(sloped, dz_ref[...])

    def load_change(from_b, from_z, r, s):
        change = []
        for c in range(3):
            change.append(
                [
                    from_b[pl.ds(pl.multiple_of(c * 2 * NQ + r, 16), 16), s],
                    from_b[pl.ds(pl.multiple_of(c * 2 * NQ + NQ + r, 16), 16), s],
                    from_z[pl.ds(pl.multiple_of(c * NQ + r, 16), 16), s],
                ]
            )
        return change

    pairs = [(0, 0), (1, 1), (2, 2), (0, 1), (0, 2), (1, 2)]

    def fluxes(first):
        def body(i, carry):
            r = pl.multiple_of(i * 16, 16)
            for half in range(2):
                s = pl.ds(half * 128, 128)
                w = weight[pl.ds(r, 16), s]
                if first:
                    grad = load_change(gsb, gsz, r, s)
                    deform = [[grad[c][a] + 1.0 if c == a else grad[c][a] for a in range(3)] for c in range(3)]
                    cg = [sum(deform[k][a] * deform[k][b] for k in range(3)) for a, b in pairs]
                    trace = (0.5 * LAME_FIRST) * (cg[0] + cg[1] + cg[2]) - 1.5 * LAME_FIRST
                    stress = [LAME_SHEAR * t for t in cg]
                    stress = [w * (t - LAME_SHEAR + trace) for t in stress[:3]] + [w * t for t in stress[3:]]
                    for c in range(3):
                        for a in range(3):
                            deform_s[3 * c + a, pl.ds(r, 16), s] = deform[c][a]
                    for k in range(6):
                        stress_s[k, pl.ds(r, 16), s] = stress[k]
                else:
                    deform = [[deform_s[3 * c + a, pl.ds(r, 16), s] for a in range(3)] for c in range(3)]
                    stress = [stress_s[k, pl.ds(r, 16), s] for k in range(6)]
                change = load_change(gvb, gvz, r, s)
                diagonal = [sum(deform[k][a] * change[k][a] for k in range(3)) for a in range(3)]
                trace = LAME_FIRST * (diagonal[0] + diagonal[1] + diagonal[2])
                moved = [w * (2.0 * LAME_SHEAR * t + trace) for t in diagonal]
                shear = LAME_SHEAR * w
                for a, b in pairs[3:]:
                    moved.append(
                        shear * sum(deform[k][a] * change[k][b] + deform[k][b] * change[k][a] for k in range(3))
                    )
                at = [[0, 3, 4], [3, 1, 5], [4, 5, 2]]
                for c in range(3):
                    for a in range(3):
                        entry = sum(change[c][b] * stress[at[b][a]] + deform[c][b] * moved[at[b][a]] for b in range(3))
                        high, low = split(entry)
                        if a < 2:
                            place = pl.ds(pl.multiple_of(c * 2 * NQ + a * NQ + r, 16), 16)
                            fbh[place, s] = high
                            fbl[place, s] = low
                        else:
                            place = pl.ds(pl.multiple_of(c * NQ + r, 16), 16)
                            fzh[place, s] = high
                            fzl[place, s] = low
            return carry

        lax.fori_loop(0, NQ // 16, body, 0)

    def divergence():
        both_b = dot(fbh[...], bzt_ref[...])
        both_z = dot(fzh[...], dzt_ref[...])
        side_b = both_b[:, :lanes] + both_b[:, lanes:] + dot(fbl[...], bzt_ref[:, :lanes])
        side_z = both_z[:, :lanes] + both_z[:, lanes:] + dot(fzl[...], dzt_ref[:, :lanes])
        columns = [
            jnp.concatenate([side_b[c * 2 * NQ : (c + 1) * 2 * NQ], side_z[c * NQ : (c + 1) * NQ]], axis=0)
            for c in range(3)
        ]
        return times_left(crosst_ref[...], jnp.concatenate(columns, axis=1))

    vertex_of_row = lax.rem(iota((48, vertices), 0), 8)
    vertex_mask = vertex_of_row == iota((48, vertices), 1) // count_z

    def restrict(field):
        rows = times_left(hats_ref[...], field)
        rows = jnp.concatenate([rows[:, c * lanes : (c + 1) * lanes] for c in range(3)], axis=0)
        rows = jnp.where(vertex_mask, times_right(rows, hatz_ref[...]), 0.0)
        rows = [jnp.sum(rows[8 * i : 8 * i + 8], axis=0, keepdims=True) for i in range(6)]
        fill = jnp.zeros((5, vertices), F32)
        return (
            jnp.concatenate([rows[0], rows[2], rows[4], fill], axis=0),
            jnp.concatenate([rows[1], rows[3], rows[5], fill], axis=0),
        )

    def widened(own, beyond):
        return jnp.concatenate([jnp.concatenate([own[c], beyond[c]], axis=0) for c in range(3)], axis=1)

    own_state = [state_ref[c].reshape(4 * ny, lanes) for c in range(3)]
    own_direction = [direction_ref[c].reshape(4 * ny, lanes) for c in range(3)]
    own_rhs = [rhs_ref[c].reshape(4 * ny, lanes) for c in range(3)]

    copy_state.wait_recv()
    beyond_state = [jnp.where(is_last, 0.0, halo_state[c]) for c in range(3)]
    gradients(widened(own_state, beyond_state), gsb, gsz)
    copy_halo.wait_recv()
    beyond_direction = [jnp.where(is_last, 0.0, halo_rx[c * ny : (c + 1) * ny, :]) for c in range(3)]
    keep_right = halo_rx[3 * ny : 4 * ny, :]
    owner_right = halo_rx[4 * ny : 4 * ny + 1, :].astype(jnp.int32)
    right_hot = (owner_right == iota((vertices, vertices), 0)).astype(F32).astype(BF16)
    gradients(widened([keep * own_direction[c] for c in range(3)], beyond_direction), gvb, gvz)
    fluxes(True)
    image = divergence()

    def settle(image, field):
        own, beyond = [], []
        for c in range(3):
            part = image[:, c * lanes : (c + 1) * lanes]
            own.append(own_rhs[c] - keep * part[: 4 * ny] - (1.0 - keep) * field[c])
            beyond.append(-keep_right * part[4 * ny :])
        return own, beyond

    own_first, beyond_first = settle(image, own_direction)
    low_sums, high_sums = restrict(widened(own_first, beyond_first))
    high_sums = jnp.where(is_last, 0.0, high_sums)
    sums_tx[0] = stacked_exact(low_sums, own_hot, dot_nt)
    sums_tx[1] = stacked_exact(high_sums, right_hot, dot_nt)

    def send_own(d):
        p = lax.rem(g + d, groups)
        remote(
            sums_tx.at[0, pl.ds(0, 4)], sums_rx.at[g, pl.ds(0, 4)], sums_send.at[d], sums_recv.at[g], (p, m)
        ).start()

    def send_next(d):
        p = lax.rem(g_right + d, groups)
        remote(
            sums_tx.at[1, pl.ds(0, 4)],
            sums_rx.at[groups + g_right, pl.ds(0, 4)],
            sums_send.at[groups + d],
            sums_recv.at[groups + g_right],
            (p, m_right),
        ).start()

    each(0, groups, send_next)
    each(1, groups, send_own)
    sums_rx[g] = sums_tx[0]

    def got_own(d):
        p = lax.rem(g + d, groups)
        remote(
            sums_tx.at[0, pl.ds(0, 4)], sums_rx.at[p, pl.ds(0, 4)], sums_send.at[d], sums_recv.at[p], (p, m)
        ).wait()

    def got_next(p):
        remote(
            sums_tx.at[1, pl.ds(0, 4)],
            sums_rx.at[groups + p, pl.ds(0, 4)],
            sums_send.at[groups + p],
            sums_recv.at[groups + p],
            right,
        ).wait()

    each(1, groups, got_own)
    each(0, groups, got_next)

    wide = inv_high.shape[2]
    received = sums_rx[:groups] + sums_rx[groups:]
    received = received.reshape(groups * 8, vertices)
    pick = (
        iota((vertices, wide), 0) == g * message + lax.rem(iota((vertices, wide), 1), message)
    ).astype(F32).astype(BF16)
    placed = stacked_exact(received, pick, dot)
    shape = (groups * 8, wide)
    row, lane = iota(shape, 0), iota(shape, 1)
    placed = jnp.where(
        (lane // block == lax.rem(row, 8))
        & (lax.rem(lane, block) // message == lax.rem(row // 8, per_block))
        & (lane < size),
        placed,
        0.0,
    )
    vectors = [
        jnp.sum(placed[b * per_block * 8 : (b + 1) * per_block * 8], axis=0, keepdims=True) for b in range(blocks)
    ]
    for b in range(blocks):
        high, low = split(jnp.broadcast_to(vectors[b], (8, wide)))
        both = dot_nt(jnp.concatenate([high, low], axis=0), inv_high[b])
        solved_tx[b] = (both[:1] + both[8:9]) + dot_nt(jnp.concatenate([high, high], axis=0), inv_low[b])[:1]

    def return_own(d):
        p = lax.rem(g + d, groups)
        remote(
            solved_tx.at[p // per_block], solved_rx.at[g], solved_send.at[d], solved_recv.at[g], (p, m)
        ).start()

    def return_left(d):
        p = lax.rem(g + d, groups)
        before = lax.rem(p + groups - at_start.astype(jnp.int32), groups)
        remote(
            solved_tx.at[p // per_block],
            solved_rx.at[groups + g],
            solved_send.at[groups + d],
            solved_recv.at[groups + g],
            (before, m_left),
        ).start()

    each(0, groups, return_left)
    each(1, groups, return_own)
    solved_rx[g] = solved_tx[g // per_block]

    def back_own(d):
        p = lax.rem(g + d, groups)
        remote(solved_tx.at[0], solved_rx.at[p], solved_send.at[d], solved_recv.at[p], (p, m)).wait()

    def back_next(p):
        remote(
            solved_tx.at[0], solved_rx.at[groups + p], solved_send.at[groups + p], solved_recv.at[groups + p], right
        ).wait()

    each(1, groups, back_own)
    each(0, groups, back_next)

    def corrections(start, group, hot):
        rows = -(-groups // 8) * 8
        at_row = iota((rows, wide), 0)
        gathered = jnp.zeros((rows, wide), F32)
        for p in range(groups):
            gathered = jnp.where(at_row == p, jnp.broadcast_to(solved_rx[start + p], (rows, wide)), gathered)
        shape = (wide, vertices)
        slots = []
        inside = iota((rows, vertices), 0) == iota((rows, vertices), 1) // message
        for c in range(3):
            base = c * block + lax.rem(group, per_block) * message
            chosen = (iota(shape, 0) == base + lax.rem(iota(shape, 1), message)).astype(F32).astype(BF16)
            slots.append(
                jnp.sum(jnp.where(inside, stacked_exact(gathered, chosen, dot), 0.0), axis=0, keepdims=True)
            )
        slots = jnp.concatenate(slots + [jnp.zeros((5, vertices), F32)], axis=0)
        return stacked_exact(slots, hot, dot)

    own_correction = corrections(0, g, own_hot)
    next_correction = jnp.where(is_last, 0.0, corrections(groups, g_right, right_hot))
    rows = []
    for c in range(3):
        rows.append(jnp.broadcast_to(own_correction[c : c + 1], (8, vertices)))
        rows.append(jnp.broadcast_to(next_correction[c : c + 1], (8, vertices)))
    rows = jnp.where(vertex_mask, jnp.concatenate(rows, axis=0), 0.0)
    rows = times_right(rows, hatzp_ref[...])
    rows = jnp.concatenate([rows[16 * c : 16 * c + 16] for c in range(3)], axis=1)
    update = times_left(hatst_ref[...], rows)
    new_direction, beyond_new = [], []
    for c in range(3):
        part = update[:, c * lanes : (c + 1) * lanes]
        new_direction.append(own_direction[c] + keep * part[: 4 * ny])
        beyond_new.append(beyond_direction[c] + keep_right * part[4 * ny :])
        new_ref[c] = new_direction[c].reshape(4, ny, lanes)
    beyond_new = [jnp.where(is_last, 0.0, t) for t in beyond_new]
    gradients(widened([keep * t for t in new_direction], beyond_new), gvb, gvz)
    fluxes(False)
    image = divergence()
    for c in range(3):
        last_tx[c * ny : (c + 1) * ny, :] = image[4 * ny :, c * lanes : (c + 1) * lanes]
    copy_layer = remote(
        last_tx.at[pl.ds(0, 3 * ny)], last_rx.at[pl.ds(0, 3 * ny)], last_send.at[0], last_recv.at[0], right
    )
    copy_layer.start()
    own_last, beyond_last = settle(image, new_direction)
    low_sums, high_sums = restrict(widened(own_last, beyond_last))
    last_tx[3 * ny :, :] = high_sums
    copy_sums = remote(
        last_tx.at[pl.ds(3 * ny, 8)], last_rx.at[pl.ds(3 * ny, 8)], last_send.at[1], last_recv.at[1], right
    )
    copy_sums.start()
    for c in range(3):
        residual_ref[c, 1:] = own_last[c][ny:].reshape(3, ny, lanes)
    copy_layer.wait_recv()
    for c in range(3):
        arrived = jnp.where(is_first, 0.0, last_rx[c * ny : (c + 1) * ny, :])
        residual_ref[c, 0] = own_last[c][:ny] - keep[:ny] * arrived
    copy_sums.wait_recv()
    total = low_sums + jnp.where(is_first, 0.0, last_rx[3 * ny :, :])
    for c in range(3):
        for k in range(count_y):
            coarse_ref[c, 0, k : k + 1, :] = total[c : c + 1, k * count_z : (k + 1) * count_z]
    copy_state.wait_send()
    copy_halo.wait_send()
    copy_layer.wait_send()
    copy_sums.wait_send()


def shards(groups, members, state, direction, rhs, clamp, stiffness, coarse_owner, coarse_inverse):
    count_y, count_z = stiffness.shape[1:]
    ny, nz = 4 * count_y, 4 * count_z
    tables = [jnp.asarray(t) for t in constant_tables(count_y, count_z)]
    blocks, size = coarse_inverse.shape[1:3]
    wide = -(-size // 128) * 128
    vmem = pl.BlockSpec(memory_space=pltpu.VMEM)
    vertices = count_y * count_z
    new, residual, coarse = pl.pallas_call(
        functools.partial(kernel, groups, members),
        out_shape=(
            jax.ShapeDtypeStruct(state.shape, F32),
            jax.ShapeDtypeStruct(state.shape, F32),
            jax.ShapeDtypeStruct((3, 1, count_y, count_z), F32),
        ),
        in_specs=[vmem] * (7 + len(tables)),
        out_specs=(vmem, vmem, vmem),
        scratch_shapes=[
            pltpu.VMEM((4 * ny + 8, nz), F32),
            pltpu.VMEM((3, ny, nz), F32),
            pltpu.VMEM((4 * ny + 8, nz), F32),
            pltpu.VMEM((2, 8, vertices), F32),
            pltpu.VMEM((2 * groups, 8, vertices), F32),
            pltpu.VMEM((blocks, 1, wide), F32),
            pltpu.VMEM((2 * groups, 1, wide), F32),
            pltpu.VMEM((3 * ny + 8, nz), F32),
            pltpu.VMEM((3 * ny + 8, nz), F32),
            pltpu.VMEM((blocks, wide, wide), BF16),
            pltpu.VMEM((blocks, wide, wide), BF16),
            pltpu.VMEM((NQ, 256), F32),
            pltpu.VMEM((6 * NQ, 256), F32),
            pltpu.VMEM((3 * NQ, 256), F32),
            pltpu.VMEM((6 * NQ, 256), F32),
            pltpu.VMEM((3 * NQ, 256), F32),
            pltpu.VMEM((9, NQ, 256), F32),
            pltpu.VMEM((6, NQ, 256), F32),
            pltpu.VMEM((6 * NQ, 256), BF16),
            pltpu.VMEM((6 * NQ, 256), BF16),
            pltpu.VMEM((3 * NQ, 256), BF16),
            pltpu.VMEM((3 * NQ, 256), BF16),
            pltpu.SemaphoreType.DMA((2,)),
            pltpu.SemaphoreType.DMA((2,)),
            pltpu.SemaphoreType.DMA((2 * groups,)),
            pltpu.SemaphoreType.DMA((2 * groups,)),
            pltpu.SemaphoreType.DMA((2 * groups,)),
            pltpu.SemaphoreType.DMA((2 * groups,)),
            pltpu.SemaphoreType.DMA((2,)),
            pltpu.SemaphoreType.DMA((2,)),
        ],
        compiler_params=pltpu.CompilerParams(
            collective_id=0, has_side_effects=True, vmem_limit_bytes=40 * 1024 * 1024
        ),
    )(state, direction, rhs, clamp, stiffness, coarse_owner, coarse_inverse, *tables)
    return (new, residual, coarse)


def solution(mesh):
    in_specs = (
        P(None, ("grp", "mem"), None, None),
        P(None, ("grp", "mem"), None, None),
        P(None, ("grp", "mem"), None, None),
        P(("grp", "mem"), None),
        P(("grp", "mem"), None, None),
        P(("grp", "mem"), None),
        P(("grp", "mem"), None, None, None),
    )
    out_specs = (
        P(None, ("grp", "mem"), None, None),
        P(None, ("grp", "mem"), None, None),
        P(None, ("grp", "mem"), None, None),
    )
    body = functools.partial(shards, mesh.shape["grp"], mesh.shape["mem"])
    return jax.shard_map(body, mesh=mesh, in_specs=in_specs, out_specs=out_specs, check_vma=False)
```

```python
import functools

import jax
import jax.numpy as jnp
import ml_dtypes
import numpy as np
from jax import lax
from jax.experimental import pallas as pl
from jax.experimental.pallas import tpu as pltpu
from jax.sharding import PartitionSpec as P

LAME_FIRST = 1.2
LAME_SHEAR = 0.8
HIGHEST = lax.Precision.HIGHEST
MESH = pl.DeviceIdType.MESH
F32 = jnp.float32
BF16 = jnp.bfloat16
INPUTS = 18
NQ = 112


def gauss_rule():
    inner = np.sqrt(5.0 - 2.0 * np.sqrt(10.0 / 7.0)) / 3.0
    outer = np.sqrt(5.0 + 2.0 * np.sqrt(10.0 / 7.0)) / 3.0
    inner_weight = (322.0 + 13.0 * np.sqrt(70.0)) / 900.0
    outer_weight = (322.0 - 13.0 * np.sqrt(70.0)) / 900.0
    points = np.array([-outer, -inner, 0.0, inner, outer])
    weights = np.array([outer_weight, inner_weight, 128.0 / 225.0, inner_weight, outer_weight])
    return (points, weights)


def basis_tables():
    gll_points = np.array([-1.0, -np.sqrt(3.0 / 7.0), 0.0, np.sqrt(3.0 / 7.0), 1.0])
    gauss_points, gauss_weights = gauss_rule()
    values = np.zeros((5, 5))
    slopes = np.zeros((5, 5))
    for j in range(5):
        others = [gll_points[k] for k in range(5) if k != j]
        denominator = np.prod([gll_points[j] - o for o in others])
        for q in range(5):
            t = gauss_points[q]
            values[q, j] = np.prod([t - o for o in others]) / denominator
            total = 0.0
            for i in range(4):
                total += np.prod([t - others[k] for k in range(4) if k != i])
            slopes[q, j] = 2.0 * total / denominator
    return (gll_points, gauss_weights, values, slopes)


def banded(table, count):
    banded_matrix = np.zeros((5 * count, 4 * count + 1))
    for e in range(count):
        banded_matrix[5 * e : 5 * e + 5, 4 * e : 4 * e + 5] = table
    return banded_matrix[:, :-1]


def restrictor(gll_points, count):
    result = np.zeros((count, 4 * count))
    for e in range(count):
        for j in range(4):
            result[e, 4 * e + j] += (1.0 - gll_points[j]) / 2.0
            if e + 1 < count:
                result[e + 1, 4 * e + j] += (1.0 + gll_points[j]) / 2.0
    return result


def halves(table):
    high = table.astype(ml_dtypes.bfloat16)
    low = (table - high.astype(np.float64)).astype(ml_dtypes.bfloat16)
    return high, low


def padded(table, axis, multiple):
    widths = [(0, 0), (0, 0)]
    widths[axis] = (0, -table.shape[axis] % multiple)
    return np.pad(table, widths)


def left_table(table):
    high, low = halves(table)
    return padded(np.concatenate([high, high, low], axis=1), 1, 128)


def right_table(table):
    high, low = halves(table)
    return np.concatenate([high, high, low], axis=0)


def constant_tables(count_y, count_z):
    gll_points, weights, values, slopes = basis_tables()
    by, dy = banded(values, count_y), banded(slopes, count_y)
    bz, dz = banded(values, count_z), banded(slopes, count_z)
    pads = lambda t: np.pad(t, ((0, NQ - t.shape[0]), (0, 0)))
    cross = np.concatenate(
        [pads(np.kron(slopes, by)), pads(np.kron(values, dy)), pads(np.kron(values, by))]
    )
    bz, dz = padded(bz, 0, 256), padded(dz, 0, 256)
    low_hat = np.append((1.0 - gll_points[:4]) / 2.0, 0.0)
    high_hat = np.append((1.0 + gll_points[:4]) / 2.0, 1.0)
    hat_y = restrictor(gll_points, count_y)
    hat_z = restrictor(gll_points, count_z)
    hats = np.zeros((16, 20 * count_y))
    hats[:count_y] = np.kron(low_hat[None], hat_y)
    hats[8 : 8 + count_y] = np.kron(high_hat[None], hat_y)
    tiled = np.tile(hat_z, (count_y, 1))
    spread_y = np.zeros((NQ, count_y))
    spread_y[:100] = np.kron(weights[:, None], np.kron(np.eye(count_y), weights[:, None])) / 8.0
    spread_z = padded(np.kron(np.eye(count_z), weights[None]), 1, 256)
    return (
        left_table(cross),
        right_table(np.concatenate([bz.T, dz.T], axis=1)),
        np.concatenate(halves(bz), axis=1),
        np.concatenate(halves(dz), axis=1),
        left_table(cross.T),
        left_table(hats),
        right_table(tiled.T),
        right_table(tiled),
        left_table(hats.T),
        spread_y.astype(np.float32),
        spread_z.astype(np.float32),
    )


def split(x):
    high = x.astype(BF16)
    return high, (x - high.astype(F32)).astype(BF16)


def dot(a, b):
    return lax.dot_general(a, b, (((1,), (0,)), ((), ())), preferred_element_type=F32)


def dot_nt(a, b):
    return lax.dot_general(a, b, (((1,), (1,)), ((), ())), preferred_element_type=F32)


def times_right(x, table):
    high, low = split(x)
    return dot(jnp.concatenate([high, low, high], axis=1), table)


def times_left(table, x):
    high, low = split(x)
    parts = [high, low, high]
    rest = table.shape[1] - 3 * x.shape[0]
    if rest:
        parts.append(jnp.zeros((rest, x.shape[1]), BF16))
    return dot(table, jnp.concatenate(parts, axis=0))


def stacked_exact(x, one_hot, product):
    rows = x.shape[0]
    high, low = split(x)
    both = product(jnp.concatenate([high, low], axis=0), one_hot)
    return both[:rows] + both[rows:]


def iota(shape, axis):
    return lax.broadcasted_iota(jnp.int32, shape, axis)


def each(low, high, act):
    if high - low <= 8:
        for i in range(low, high):
            act(i)
    else:

        def step(i, carry):
            act(i)
            return carry

        lax.fori_loop(low, high, step, 0)


def kernel(groups, members, *refs):
    sources, outputs = refs[:INPUTS], refs[INPUTS : INPUTS + 3]
    local, scratch = refs[INPUTS + 3 : 2 * INPUTS + 3], refs[2 * INPUTS + 3 :]
    state_ref, direction_ref, rhs_ref, clamp_ref, stiff_ref, owner_ref, inverse_ref = local[:7]
    spready_ref, spreadz_ref = local[16:]
    new_ref, residual_ref, coarse_ref = scratch[:3]
    narrow = scratch[3:12]
    cross_ref, bdz_ref, bzt_ref, dzt_ref, crosst_ref, hats_ref, hatz_ref, hatzp_ref, hatst_ref = narrow
    (
        halo_tx,
        halo_state,
        halo_rx,
        sums_tx,
        sums_rx,
        solved_tx,
        solved_rx,
        last_tx,
        last_rx,
        inv_high,
        inv_low,
        weight,
        gsb,
        gsz,
        gvb,
        gvz,
        deform_s,
        stress_s,
        fbh,
        fbl,
        fzh,
        fzl,
        halo_send,
        halo_recv,
        sums_send,
        sums_recv,
        solved_send,
        solved_recv,
        last_send,
        last_recv,
        load_sem,
        store_sem,
    ) = scratch[12:]
    count_y, count_z = stiff_ref.shape[1:]
    ny = 4 * count_y
    vertices = count_y * count_z
    blocks = inverse_ref.shape[1]
    size = inverse_ref.shape[2]
    block = size // 3
    message = vertices // groups
    per_block = groups // blocks
    g = lax.axis_index("grp")
    m = lax.axis_index("mem")
    m_right = lax.rem(m + 1, members)
    m_left = lax.rem(m + members - 1, members)
    at_end = m == members - 1
    at_start = m == 0
    g_right = lax.rem(g + at_end.astype(jnp.int32), groups)
    g_left = lax.rem(g + groups - at_start.astype(jnp.int32), groups)
    is_last = (g * members + m) == groups * members - 1
    is_first = (g * members + m) == 0

    barrier = pltpu.get_barrier_semaphore()

    def greet(p, member):
        pl.semaphore_signal(barrier, inc=1, device_id=(p, member), device_id_type=MESH)

    greet(g_left, m_left)
    each(1, groups, lambda d: greet(lax.rem(g_left + d, groups), m_left))
    each(0, groups, lambda d: greet(lax.rem(g_right + d, groups), m_right))
    each(1, groups, lambda d: greet(lax.rem(g + d, groups), m))
    loads = [pltpu.make_async_copy(a, b, load_sem.at[i]) for i, (a, b) in enumerate(zip(sources, local))]
    order = [3, 5, 1, 0, 6, 4, 16, 17, 8, 7]
    for i in order + [i for i in range(INPUTS) if i not in order]:
        loads[i].start()

    def loaded(*which):
        for i in which:
            loads[i].wait()
            if 7 <= i < 16:
                narrow[i - 7][...] = local[i][...].astype(BF16)

    loaded(3, 5, 1)

    eye = iota((ny, ny), 0) == iota((ny, ny), 1)
    clamp_rows = []
    for x in range(4):
        row = jnp.broadcast_to(clamp_ref[x : x + 1, :].astype(F32), (ny, ny))
        clamp_rows.append(jnp.sum(jnp.where(eye, row, 0.0), axis=1, keepdims=True))
    clamped = jnp.concatenate(clamp_rows, axis=0)
    lanes = 4 * count_z
    keep = jnp.where(iota((4 * ny, lanes), 1) == 0, 1.0 - clamped, 1.0)
    for c in range(3):
        halo_tx[c * ny : (c + 1) * ny, :] = keep[:ny] * direction_ref[c, 0]
    halo_tx[3 * ny : 4 * ny, :] = keep[:ny]
    halo_tx[4 * ny : 4 * ny + 8, :] = jnp.broadcast_to(owner_ref[...].astype(F32), (8, vertices))
    pl.semaphore_wait(barrier, 3 * groups - 1)

    def along_z(parts):
        return times_right(jnp.concatenate(parts, axis=0), bdz_ref[...])

    left = (g_left, m_left)
    right = (g_right, m_right)

    def remote(src, dst, send, recv, device):
        return pltpu.make_async_remote_copy(
            src_ref=src, dst_ref=dst, send_sem=send, recv_sem=recv, device_id=device, device_id_type=MESH
        )

    copy_state = remote(sources[0].at[:, 0], halo_state, halo_send.at[0], halo_recv.at[0], left)
    copy_state.start()
    copy_halo = remote(halo_tx, halo_rx, halo_send.at[1], halo_recv.at[1], left)
    copy_halo.start()

    loaded(0, 8)
    own_state = [state_ref[c].reshape(4 * ny, lanes) for c in range(3)]
    own_direction = [direction_ref[c].reshape(4 * ny, lanes) for c in range(3)]
    state_z = along_z(own_state)
    direction_z = along_z([keep * t for t in own_direction])
    sums_rx[:, 4:, :] = jnp.zeros((2 * groups, 4, vertices), F32)
    loaded(6, 4, 16, 17)
    inv_high[...] = jnp.zeros_like(inv_high)
    inv_low[...] = jnp.zeros_like(inv_low)
    for b in range(blocks):
        high, low = split(inverse_ref[0, b])
        inv_high[b, :size, :size] = high
        inv_low[b, :size, :size] = low
    along_y = jnp.zeros((NQ, count_z), F32)
    for k in range(count_y):
        along_y = along_y + spready_ref[:, k : k + 1] * stiff_ref[0, k : k + 1, :]
    weight[...] = jnp.dot(along_y, spreadz_ref[...], precision=HIGHEST, preferred_element_type=F32)
    own_hot = (owner_ref[...] == iota((vertices, vertices), 0)).astype(F32).astype(BF16)

    wide = inv_high.shape[2]
    pick = (
        iota((vertices, wide), 0) == g * message + lax.rem(iota((vertices, wide), 1), message)
    ).astype(F32).astype(BF16)
    shape = (groups * 8, wide)
    row, lane = iota(shape, 0), iota(shape, 1)
    pick_mask = (
        (lane // block == lax.rem(row, 8))
        & (lax.rem(lane, block) // message == lax.rem(row // 8, per_block))
        & (lane < size)
    )
    owner_rows = -(-groups // 8) * 8

    def choices(owner, group):
        place = lax.rem(group, per_block) * message + lax.rem(owner, message)
        rows = iota((wide, vertices), 0)
        chosen = jnp.concatenate([rows == c * block + place for c in range(3)], axis=1)
        return chosen.astype(F32).astype(BF16), iota((owner_rows, vertices), 0) == owner // message

    own_choices = choices(owner_ref[...], g)

    def gradients(own, beyond, to_b, to_z):
        parts = []
        for first in (0, 256):
            columns = [
                jnp.concatenate(
                    [
                        own[c * 4 * ny : (c + 1) * 4 * ny, first : first + 256],
                        beyond[c * ny : (c + 1) * ny, first : first + 256],
                    ],
                    axis=0,
                )
                for c in range(3)
            ]
            parts.append(jnp.concatenate(columns, axis=1))
        to_b[...] = times_left(cross_ref[: 2 * NQ, :], parts[0])
        to_z[...] = times_left(cross_ref[2 * NQ :, :], parts[1])

    def load_change(from_b, from_z, r, half):
        change = []
        for c in range(3):
            s = pl.ds(c * 256 + half * 128, 128)
            change.append(
                [
                    from_b[pl.ds(r, 16), s],
                    from_b[pl.ds(pl.multiple_of(NQ + r, 16), 16), s],
                    from_z[pl.ds(r, 16), s],
                ]
            )
        return change

    pairs = [(0, 0), (1, 1), (2, 2), (0, 1), (0, 2), (1, 2)]

    def fluxes(first):
        def body(i, carry):
            r = pl.multiple_of(i * 16, 16)
            for half in range(2):
                s = pl.ds(half * 128, 128)
                w = weight[pl.ds(r, 16), s]
                if first:
                    grad = load_change(gsb, gsz, r, half)
                    deform = [[grad[c][a] + 1.0 if c == a else grad[c][a] for a in range(3)] for c in range(3)]
                    cg = [sum(deform[k][a] * deform[k][b] for k in range(3)) for a, b in pairs]
                    trace = (0.5 * LAME_FIRST) * (cg[0] + cg[1] + cg[2]) - 1.5 * LAME_FIRST
                    stress = [LAME_SHEAR * t for t in cg]
                    stress = [w * (t - LAME_SHEAR + trace) for t in stress[:3]] + [w * t for t in stress[3:]]
                    for c in range(3):
                        for a in range(3):
                            deform_s[3 * c + a, pl.ds(r, 16), s] = deform[c][a]
                    for k in range(6):
                        stress_s[k, pl.ds(r, 16), s] = stress[k]
                else:
                    deform = [[deform_s[3 * c + a, pl.ds(r, 16), s] for a in range(3)] for c in range(3)]
                    stress = [stress_s[k, pl.ds(r, 16), s] for k in range(6)]
                change = load_change(gvb, gvz, r, half)
                diagonal = [sum(deform[k][a] * change[k][a] for k in range(3)) for a in range(3)]
                trace = LAME_FIRST * (diagonal[0] + diagonal[1] + diagonal[2])
                moved = [w * (2.0 * LAME_SHEAR * t + trace) for t in diagonal]
                shear = LAME_SHEAR * w
                for a, b in pairs[3:]:
                    moved.append(
                        shear * sum(deform[k][a] * change[k][b] + deform[k][b] * change[k][a] for k in range(3))
                    )
                at = [[0, 3, 4], [3, 1, 5], [4, 5, 2]]
                for c in range(3):
                    for a in range(3):
                        entry = sum(change[c][b] * stress[at[b][a]] + deform[c][b] * moved[at[b][a]] for b in range(3))
                        high, low = split(entry)
                        if a < 2:
                            place = pl.ds(pl.multiple_of(c * 2 * NQ + a * NQ + r, 16), 16)
                            fbh[place, s] = high
                            fbl[place, s] = low
                        else:
                            place = pl.ds(pl.multiple_of(c * NQ + r, 16), 16)
                            fzh[place, s] = high
                            fzl[place, s] = low
            return carry

        lax.fori_loop(0, NQ // 16, body, 0)

    def divergence():
        both_b = dot(fbh[...], bzt_ref[...])
        both_z = dot(fzh[...], dzt_ref[...])
        side_b = both_b[:, :lanes] + both_b[:, lanes:] + dot(fbl[...], bzt_ref[:, :lanes])
        side_z = both_z[:, :lanes] + both_z[:, lanes:] + dot(fzl[...], dzt_ref[:, :lanes])
        columns = [
            jnp.concatenate([side_b[c * 2 * NQ : (c + 1) * 2 * NQ], side_z[c * NQ : (c + 1) * NQ]], axis=0)
            for c in range(3)
        ]
        return times_left(crosst_ref[...], jnp.concatenate(columns, axis=1))

    vertex_of_row = lax.rem(iota((48, vertices), 0), 8)
    vertex_mask = vertex_of_row == iota((48, vertices), 1) // count_z

    def restrict(field):
        rows = times_left(hats_ref[...], field)
        rows = jnp.concatenate([rows[:, c * lanes : (c + 1) * lanes] for c in range(3)], axis=0)
        rows = jnp.where(vertex_mask, times_right(rows, hatz_ref[...]), 0.0)
        rows = [jnp.sum(rows[8 * i : 8 * i + 8], axis=0, keepdims=True) for i in range(6)]
        fill = jnp.zeros((5, vertices), F32)
        return (
            jnp.concatenate([rows[0], rows[2], rows[4], fill], axis=0),
            jnp.concatenate([rows[1], rows[3], rows[5], fill], axis=0),
        )

    def widened(own, beyond):
        return jnp.concatenate([jnp.concatenate([own[c], beyond[c]], axis=0) for c in range(3)], axis=1)

    loaded(*[i for i in range(INPUTS) if i not in (3, 5, 1, 0, 8, 6, 4, 16, 17)])
    own_rhs = [rhs_ref[c].reshape(4 * ny, lanes) for c in range(3)]

    copy_state.wait_recv()
    beyond_state = [jnp.where(is_last, 0.0, halo_state[c]) for c in range(3)]
    gradients(state_z, along_z(beyond_state), gsb, gsz)
    copy_halo.wait_recv()
    beyond_direction = [jnp.where(is_last, 0.0, halo_rx[c * ny : (c + 1) * ny, :]) for c in range(3)]
    keep_right = halo_rx[3 * ny : 4 * ny, :]
    owner_right = halo_rx[4 * ny : 4 * ny + 1, :].astype(jnp.int32)
    right_hot = (owner_right == iota((vertices, vertices), 0)).astype(F32).astype(BF16)
    gradients(direction_z, along_z(beyond_direction), gvb, gvz)
    right_choices = choices(owner_right, g_right)
    fluxes(True)
    image = divergence()

    def settle(image, field):
        own, beyond = [], []
        for c in range(3):
            part = image[:, c * lanes : (c + 1) * lanes]
            own.append(own_rhs[c] - keep * part[: 4 * ny] - (1.0 - keep) * field[c])
            beyond.append(-keep_right * part[4 * ny :])
        return own, beyond

    own_first, beyond_first = settle(image, own_direction)
    low_sums, high_sums = restrict(widened(own_first, beyond_first))
    high_sums = jnp.where(is_last, 0.0, high_sums)
    sums_tx[0] = stacked_exact(low_sums, own_hot, dot_nt)
    sums_tx[1] = stacked_exact(high_sums, right_hot, dot_nt)

    def send_own(d):
        p = lax.rem(g + d, groups)
        remote(
            sums_tx.at[0, pl.ds(0, 4)], sums_rx.at[g, pl.ds(0, 4)], sums_send.at[d], sums_recv.at[g], (p, m)
        ).start()

    def send_next(d):
        p = lax.rem(g_right + d, groups)
        remote(
            sums_tx.at[1, pl.ds(0, 4)],
            sums_rx.at[groups + g_right, pl.ds(0, 4)],
            sums_send.at[groups + d],
            sums_recv.at[groups + g_right],
            (p, m_right),
        ).start()

    each(0, groups, send_next)
    each(1, groups, send_own)
    sums_rx[g] = sums_tx[0]

    def got_own(d):
        p = lax.rem(g + d, groups)
        remote(
            sums_tx.at[0, pl.ds(0, 4)], sums_rx.at[p, pl.ds(0, 4)], sums_send.at[d], sums_recv.at[p], (p, m)
        ).wait()

    def got_next(p):
        remote(
            sums_tx.at[1, pl.ds(0, 4)],
            sums_rx.at[groups + p, pl.ds(0, 4)],
            sums_send.at[groups + p],
            sums_recv.at[groups + p],
            right,
        ).wait()

    each(1, groups, got_own)
    each(0, groups, got_next)

    received = sums_rx[:groups] + sums_rx[groups:]
    received = received.reshape(groups * 8, vertices)
    placed = jnp.where(pick_mask, stacked_exact(received, pick, dot), 0.0)
    vectors = [
        jnp.sum(placed[b * per_block * 8 : (b + 1) * per_block * 8], axis=0, keepdims=True) for b in range(blocks)
    ]
    for b in range(blocks):
        high, low = split(jnp.broadcast_to(vectors[b], (8, wide)))
        both = dot_nt(jnp.concatenate([high, low], axis=0), inv_high[b])
        solved_tx[b] = (both[:1] + both[8:9]) + dot_nt(jnp.concatenate([high, high], axis=0), inv_low[b])[:1]

    def return_own(d):
        p = lax.rem(g + d, groups)
        remote(
            solved_tx.at[p // per_block], solved_rx.at[g], solved_send.at[d], solved_recv.at[g], (p, m)
        ).start()

    def return_left(d):
        p = lax.rem(g + d, groups)
        before = lax.rem(p + groups - at_start.astype(jnp.int32), groups)
        remote(
            solved_tx.at[p // per_block],
            solved_rx.at[groups + g],
            solved_send.at[groups + d],
            solved_recv.at[groups + g],
            (before, m_left),
        ).start()

    each(0, groups, return_left)
    each(1, groups, return_own)
    solved_rx[g] = solved_tx[g // per_block]

    def back_own(d):
        p = lax.rem(g + d, groups)
        remote(solved_tx.at[0], solved_rx.at[p], solved_send.at[d], solved_recv.at[p], (p, m)).wait()

    def back_next(p):
        remote(
            solved_tx.at[0], solved_rx.at[groups + p], solved_send.at[groups + p], solved_recv.at[groups + p], right
        ).wait()

    each(1, groups, back_own)
    each(0, groups, back_next)

    def corrections(start, chosen, mask):
        at_row = iota((owner_rows, wide), 0)
        gathered = jnp.zeros((owner_rows, wide), F32)
        for p in range(groups):
            gathered = jnp.where(at_row == p, jnp.broadcast_to(solved_rx[start + p], gathered.shape), gathered)
        values = stacked_exact(gathered, chosen, dot)
        values = [values[:, c * vertices : (c + 1) * vertices] for c in range(3)]
        return [jnp.sum(jnp.where(mask, t, 0.0), axis=0, keepdims=True) for t in values]

    own_correction = corrections(0, *own_choices)
    next_correction = [jnp.where(is_last, 0.0, t) for t in corrections(groups, *right_choices)]
    rows = []
    for c in range(3):
        rows.append(jnp.broadcast_to(own_correction[c], (8, vertices)))
        rows.append(jnp.broadcast_to(next_correction[c], (8, vertices)))
    rows = jnp.where(vertex_mask, jnp.concatenate(rows, axis=0), 0.0)
    rows = times_right(rows, hatzp_ref[...])
    rows = jnp.concatenate([rows[16 * c : 16 * c + 16] for c in range(3)], axis=1)
    update = times_left(hatst_ref[...], rows)
    new_direction, beyond_new = [], []
    for c in range(3):
        part = update[:, c * lanes : (c + 1) * lanes]
        new_direction.append(own_direction[c] + keep * part[: 4 * ny])
        beyond_new.append(beyond_direction[c] + keep_right * part[4 * ny :])
        new_ref[c] = new_direction[c].reshape(4, ny, lanes)
    store_new = pltpu.make_async_copy(new_ref, outputs[0], store_sem.at[0])
    store_new.start()
    beyond_new = [jnp.where(is_last, 0.0, t) for t in beyond_new]
    gradients(along_z([keep * t for t in new_direction]), along_z(beyond_new), gvb, gvz)
    fluxes(False)
    image = divergence()
    for c in range(3):
        last_tx[c * ny : (c + 1) * ny, :] = image[4 * ny :, c * lanes : (c + 1) * lanes]
    copy_layer = remote(
        last_tx.at[pl.ds(0, 3 * ny)], last_rx.at[pl.ds(0, 3 * ny)], last_send.at[0], last_recv.at[0], right
    )
    copy_layer.start()
    own_last, beyond_last = settle(image, new_direction)
    low_sums, high_sums = restrict(widened(own_last, beyond_last))
    last_tx[3 * ny :, :] = high_sums
    copy_sums = remote(
        last_tx.at[pl.ds(3 * ny, 8)], last_rx.at[pl.ds(3 * ny, 8)], last_send.at[1], last_recv.at[1], right
    )
    copy_sums.start()
    for c in range(3):
        residual_ref[c, 1:] = own_last[c][ny:].reshape(3, ny, lanes)
    store_rest = pltpu.make_async_copy(residual_ref.at[:, 1:], outputs[1].at[:, 1:], store_sem.at[1])
    store_rest.start()
    copy_layer.wait_recv()
    for c in range(3):
        arrived = jnp.where(is_first, 0.0, last_rx[c * ny : (c + 1) * ny, :])
        residual_ref[c, 0] = own_last[c][:ny] - keep[:ny] * arrived
    store_first = pltpu.make_async_copy(residual_ref.at[:, 0], outputs[1].at[:, 0], store_sem.at[2])
    store_first.start()
    copy_sums.wait_recv()
    total = low_sums + jnp.where(is_first, 0.0, last_rx[3 * ny :, :])
    for c in range(3):
        for k in range(count_y):
            coarse_ref[c, 0, k : k + 1, :] = total[c : c + 1, k * count_z : (k + 1) * count_z]
    store_coarse = pltpu.make_async_copy(coarse_ref, outputs[2], store_sem.at[3])
    store_coarse.start()
    store_new.wait()
    store_rest.wait()
    store_first.wait()
    store_coarse.wait()
    copy_state.wait_send()
    copy_halo.wait_send()
    copy_layer.wait_send()
    copy_sums.wait_send()


def write_out(new, residual, coarse, new_out, residual_out, coarse_out, sems):
    pairs = ((new, new_out), (residual, residual_out), (coarse, coarse_out))
    copies = [pltpu.make_async_copy(a, b, sems.at[i]) for i, (a, b) in enumerate(pairs)]
    for copy in copies:
        copy.start()
    for copy in copies:
        copy.wait()


def shards(groups, members, state, direction, rhs, clamp, stiffness, coarse_owner, coarse_inverse):
    count_y, count_z = stiffness.shape[1:]
    ny, nz = 4 * count_y, 4 * count_z
    tables = [jnp.asarray(t.astype(np.float32)) for t in constant_tables(count_y, count_z)]
    blocks, size = coarse_inverse.shape[1:3]
    wide = -(-size // 128) * 128
    vertices = count_y * count_z
    operands = [state, direction, rhs, clamp, stiffness, coarse_owner, coarse_inverse, *tables]
    new, residual, coarse = pl.pallas_call(
        functools.partial(kernel, groups, members),
        out_shape=(
            jax.ShapeDtypeStruct(state.shape, F32),
            jax.ShapeDtypeStruct(state.shape, F32),
            jax.ShapeDtypeStruct((3, 1, count_y, count_z), F32),
        ),
        in_specs=[pl.BlockSpec(memory_space=pl.ANY)] * INPUTS,
        out_specs=[pl.BlockSpec(memory_space=pl.ANY)] * 3,
        scratch_shapes=[pltpu.VMEM(t.shape, t.dtype) for t in operands]
        + [pltpu.VMEM(t.shape, F32) for t in (state, state, jnp.zeros((3, 1, count_y, count_z), F32))]
        + [pltpu.VMEM(t.shape, BF16) for t in tables[:9]]
        + [
            pltpu.VMEM((4 * ny + 8, nz), F32),
            pltpu.VMEM((3, ny, nz), F32),
            pltpu.VMEM((4 * ny + 8, nz), F32),
            pltpu.VMEM((2, 8, vertices), F32),
            pltpu.VMEM((2 * groups, 8, vertices), F32),
            pltpu.VMEM((blocks, 1, wide), F32),
            pltpu.VMEM((2 * groups, 1, wide), F32),
            pltpu.VMEM((3 * ny + 8, nz), F32),
            pltpu.VMEM((3 * ny + 8, nz), F32),
            pltpu.VMEM((blocks, wide, wide), BF16),
            pltpu.VMEM((blocks, wide, wide), BF16),
            pltpu.VMEM((NQ, 256), F32),
            pltpu.VMEM((2 * NQ, 768), F32),
            pltpu.VMEM((NQ, 768), F32),
            pltpu.VMEM((2 * NQ, 768), F32),
            pltpu.VMEM((NQ, 768), F32),
            pltpu.VMEM((9, NQ, 256), F32),
            pltpu.VMEM((6, NQ, 256), F32),
            pltpu.VMEM((6 * NQ, 256), BF16),
            pltpu.VMEM((6 * NQ, 256), BF16),
            pltpu.VMEM((3 * NQ, 256), BF16),
            pltpu.VMEM((3 * NQ, 256), BF16),
            pltpu.SemaphoreType.DMA((2,)),
            pltpu.SemaphoreType.DMA((2,)),
            pltpu.SemaphoreType.DMA((2 * groups,)),
            pltpu.SemaphoreType.DMA((2 * groups,)),
            pltpu.SemaphoreType.DMA((2 * groups,)),
            pltpu.SemaphoreType.DMA((2 * groups,)),
            pltpu.SemaphoreType.DMA((2,)),
            pltpu.SemaphoreType.DMA((2,)),
            pltpu.SemaphoreType.DMA((INPUTS,)),
            pltpu.SemaphoreType.DMA((4,)),
        ],
        compiler_params=pltpu.CompilerParams(
            collective_id=0, has_side_effects=True, vmem_limit_bytes=56 * 1024 * 1024
        ),
    )(*operands)
    return pl.pallas_call(
        write_out,
        out_shape=tuple(jax.ShapeDtypeStruct(t.shape, F32) for t in (new, residual, coarse)),
        in_specs=[pl.BlockSpec(memory_space=pl.ANY)] * 3,
        out_specs=[pl.BlockSpec(memory_space=pl.ANY)] * 3,
        scratch_shapes=[pltpu.SemaphoreType.DMA((3,))],
        compiler_params=pltpu.CompilerParams(vmem_limit_bytes=56 * 1024 * 1024),
    )(new, residual, coarse)


def solution(mesh):
    in_specs = (
        P(None, ("grp", "mem"), None, None),
        P(None, ("grp", "mem"), None, None),
        P(None, ("grp", "mem"), None, None),
        P(("grp", "mem"), None),
        P(("grp", "mem"), None, None),
        P(("grp", "mem"), None),
        P(("grp", "mem"), None, None, None),
    )
    out_specs = (
        P(None, ("grp", "mem"), None, None),
        P(None, ("grp", "mem"), None, None),
        P(None, ("grp", "mem"), None, None),
    )
    body = functools.partial(shards, mesh.shape["grp"], mesh.shape["mem"])
    return jax.shard_map(body, mesh=mesh, in_specs=in_specs, out_specs=out_specs, check_vma=False)
```

```python
import functools

import jax
import jax.numpy as jnp
import ml_dtypes
import numpy as np
from jax import lax
from jax.experimental import pallas as pl
from jax.experimental.pallas import tpu as pltpu
from jax.sharding import PartitionSpec as P

LAME_FIRST = 1.2
LAME_SHEAR = 0.8
HIGHEST = lax.Precision.HIGHEST
MESH = pl.DeviceIdType.MESH
F32 = jnp.float32
BF16 = jnp.bfloat16
INPUTS = 18
NQ = 112


def gauss_rule():
    inner = np.sqrt(5.0 - 2.0 * np.sqrt(10.0 / 7.0)) / 3.0
    outer = np.sqrt(5.0 + 2.0 * np.sqrt(10.0 / 7.0)) / 3.0
    inner_weight = (322.0 + 13.0 * np.sqrt(70.0)) / 900.0
    outer_weight = (322.0 - 13.0 * np.sqrt(70.0)) / 900.0
    points = np.array([-outer, -inner, 0.0, inner, outer])
    weights = np.array([outer_weight, inner_weight, 128.0 / 225.0, inner_weight, outer_weight])
    return (points, weights)


def basis_tables():
    gll_points = np.array([-1.0, -np.sqrt(3.0 / 7.0), 0.0, np.sqrt(3.0 / 7.0), 1.0])
    gauss_points, gauss_weights = gauss_rule()
    values = np.zeros((5, 5))
    slopes = np.zeros((5, 5))
    for j in range(5):
        others = [gll_points[k] for k in range(5) if k != j]
        denominator = np.prod([gll_points[j] - o for o in others])
        for q in range(5):
            t = gauss_points[q]
            values[q, j] = np.prod([t - o for o in others]) / denominator
            total = 0.0
            for i in range(4):
                total += np.prod([t - others[k] for k in range(4) if k != i])
            slopes[q, j] = 2.0 * total / denominator
    return (gll_points, gauss_weights, values, slopes)


def banded(table, count):
    banded_matrix = np.zeros((5 * count, 4 * count + 1))
    for e in range(count):
        banded_matrix[5 * e : 5 * e + 5, 4 * e : 4 * e + 5] = table
    return banded_matrix[:, :-1]


def restrictor(gll_points, count):
    result = np.zeros((count, 4 * count))
    for e in range(count):
        for j in range(4):
            result[e, 4 * e + j] += (1.0 - gll_points[j]) / 2.0
            if e + 1 < count:
                result[e + 1, 4 * e + j] += (1.0 + gll_points[j]) / 2.0
    return result


def halves(table):
    high = table.astype(ml_dtypes.bfloat16)
    low = (table - high.astype(np.float64)).astype(ml_dtypes.bfloat16)
    return high, low


def padded(table, axis, multiple):
    widths = [(0, 0), (0, 0)]
    widths[axis] = (0, -table.shape[axis] % multiple)
    return np.pad(table, widths)


def left_table(table):
    high, low = halves(table)
    return padded(np.concatenate([high, high, low], axis=1), 1, 128)


def right_table(table):
    high, low = halves(table)
    return np.concatenate([high, high, low], axis=0)


def constant_tables(count_y, count_z):
    gll_points, weights, values, slopes = basis_tables()
    by, dy = banded(values, count_y), banded(slopes, count_y)
    bz, dz = banded(values, count_z), banded(slopes, count_z)
    pads = lambda t: np.pad(t, ((0, NQ - t.shape[0]), (0, 0)))
    cross = np.concatenate(
        [pads(np.kron(slopes, by)), pads(np.kron(values, dy)), pads(np.kron(values, by))]
    )
    bz, dz = padded(bz, 0, 256), padded(dz, 0, 256)
    low_hat = np.append((1.0 - gll_points[:4]) / 2.0, 0.0)
    high_hat = np.append((1.0 + gll_points[:4]) / 2.0, 1.0)
    hat_y = restrictor(gll_points, count_y)
    hat_z = restrictor(gll_points, count_z)
    hats = np.zeros((16, 20 * count_y))
    hats[:count_y] = np.kron(low_hat[None], hat_y)
    hats[8 : 8 + count_y] = np.kron(high_hat[None], hat_y)
    tiled = np.tile(hat_z, (count_y, 1))
    spread_y = np.zeros((NQ, count_y))
    spread_y[:100] = np.kron(weights[:, None], np.kron(np.eye(count_y), weights[:, None])) / 8.0
    spread_z = padded(np.kron(np.eye(count_z), weights[None]), 1, 256)
    return (
        left_table(cross),
        right_table(np.concatenate([bz.T, dz.T], axis=1)),
        np.concatenate(halves(bz), axis=1),
        np.concatenate(halves(dz), axis=1),
        left_table(cross.T),
        left_table(hats),
        right_table(tiled.T),
        right_table(tiled),
        left_table(hats.T),
        spread_y.astype(np.float32),
        spread_z.astype(np.float32),
    )


def split(x):
    high = x.astype(BF16)
    return high, (x - high.astype(F32)).astype(BF16)


def dot(a, b):
    return lax.dot_general(a, b, (((1,), (0,)), ((), ())), preferred_element_type=F32)


def dot_nt(a, b):
    return lax.dot_general(a, b, (((1,), (1,)), ((), ())), preferred_element_type=F32)


def times_right(x, table):
    high, low = split(x)
    return dot(jnp.concatenate([high, low, high], axis=1), table)


def times_left(table, x):
    high, low = split(x)
    parts = [high, low, high]
    rest = table.shape[1] - 3 * x.shape[0]
    if rest:
        parts.append(jnp.zeros((rest, x.shape[1]), BF16))
    return dot(table, jnp.concatenate(parts, axis=0))


def stacked_exact(x, one_hot, product):
    rows = x.shape[0]
    high, low = split(x)
    both = product(jnp.concatenate([high, low], axis=0), one_hot)
    return both[:rows] + both[rows:]


def iota(shape, axis):
    return lax.broadcasted_iota(jnp.int32, shape, axis)


def each(low, high, act):
    if high - low <= 8:
        for i in range(low, high):
            act(i)
    else:

        def step(i, carry):
            act(i)
            return carry

        lax.fori_loop(low, high, step, 0)


def kernel(groups, members, *refs):
    sources, outputs = refs[:INPUTS], refs[INPUTS : INPUTS + 3]
    local, scratch = refs[INPUTS + 3 : 2 * INPUTS + 3], refs[2 * INPUTS + 3 :]
    state_ref, direction_ref, rhs_ref, clamp_ref, stiff_ref, owner_ref, inverse_ref = local[:7]
    spready_ref, spreadz_ref = local[16:]
    new_ref, residual_ref, coarse_ref = scratch[:3]
    narrow = scratch[3:12]
    cross_ref, bdz_ref, bzt_ref, dzt_ref, crosst_ref, hats_ref, hatz_ref, hatzp_ref, hatst_ref = narrow
    (
        halo_clamp,
        halo_owner,
        halo_state,
        halo_rx,
        sums_tx,
        sums_rx,
        solved_tx,
        solved_rx,
        last_tx,
        last_rx,
        inv_high,
        inv_low,
        weight,
        gsb,
        gsz,
        gvb,
        gvz,
        deform_s,
        stress_s,
        fbh,
        fbl,
        fzh,
        fzl,
        halo_send,
        halo_recv,
        sums_send,
        sums_recv,
        solved_send,
        solved_recv,
        last_send,
        last_recv,
        load_sem,
        store_sem,
    ) = scratch[12:]
    count_y, count_z = stiff_ref.shape[1:]
    ny = 4 * count_y
    vertices = count_y * count_z
    blocks = inverse_ref.shape[1]
    size = inverse_ref.shape[2]
    block = size // 3
    message = vertices // groups
    per_block = groups // blocks
    g = lax.axis_index("grp")
    m = lax.axis_index("mem")
    m_right = lax.rem(m + 1, members)
    m_left = lax.rem(m + members - 1, members)
    at_end = m == members - 1
    at_start = m == 0
    g_right = lax.rem(g + at_end.astype(jnp.int32), groups)
    g_left = lax.rem(g + groups - at_start.astype(jnp.int32), groups)
    is_last = (g * members + m) == groups * members - 1
    is_first = (g * members + m) == 0

    barrier = pltpu.get_barrier_semaphore()

    def greet(p, member):
        pl.semaphore_signal(barrier, inc=1, device_id=(p, member), device_id_type=MESH)

    greet(g_left, m_left)
    each(1, groups, lambda d: greet(lax.rem(g_left + d, groups), m_left))
    each(0, groups, lambda d: greet(lax.rem(g_right + d, groups), m_right))
    each(1, groups, lambda d: greet(lax.rem(g + d, groups), m))
    loads = [pltpu.make_async_copy(a, b, load_sem.at[i]) for i, (a, b) in enumerate(zip(sources, local))]
    order = [3, 5, 1, 0, 6, 4, 16, 17, 8, 7]
    for i in order + [i for i in range(INPUTS) if i not in order]:
        loads[i].start()

    def loaded(*which):
        for i in which:
            loads[i].wait()
            if 7 <= i < 16:
                narrow[i - 7][...] = local[i][...].astype(BF16)

    pl.semaphore_wait(barrier, 3 * groups - 1)

    def along_z(parts):
        return times_right(jnp.concatenate(parts, axis=0), bdz_ref[...])

    left = (g_left, m_left)
    right = (g_right, m_right)

    def remote(src, dst, send, recv, device):
        return pltpu.make_async_remote_copy(
            src_ref=src, dst_ref=dst, send_sem=send, recv_sem=recv, device_id=device, device_id_type=MESH
        )

    halo = [
        remote(a, b, halo_send.at[i], halo_recv.at[i], left)
        for i, (a, b) in enumerate(
            (
                (sources[0].at[:, 0], halo_state),
                (sources[1].at[:, 0], halo_rx),
                (sources[3], halo_clamp),
                (sources[5], halo_owner),
            )
        )
    ]

    @pl.when(jnp.logical_not(is_first))
    def _():
        for copy in halo:
            copy.start()

    def clamp_column(ref, x):
        row = jnp.broadcast_to(ref[x : x + 1, :].astype(F32), (ny, ny))
        return jnp.sum(jnp.where(iota((ny, ny), 0) == iota((ny, ny), 1), row, 0.0), axis=1, keepdims=True)

    def keep_of(column):
        shape = (column.shape[0], lanes)
        return jnp.where(iota(shape, 1) == 0, jnp.broadcast_to(1.0 - column, shape), 1.0)

    lanes = 4 * count_z
    loaded(3, 5, 1)
    keep = keep_of(jnp.concatenate([clamp_column(clamp_ref, x) for x in range(4)], axis=0))

    loaded(0, 8)
    own_state = [state_ref[c].reshape(4 * ny, lanes) for c in range(3)]
    own_direction = [direction_ref[c].reshape(4 * ny, lanes) for c in range(3)]
    state_z = along_z(own_state)
    direction_z = along_z([keep * t for t in own_direction])
    sums_rx[:, 4:, :] = jnp.zeros((2 * groups, 4, vertices), F32)
    loaded(4, 16, 17, 7)
    along_y = jnp.zeros((NQ, count_z), F32)
    for k in range(count_y):
        along_y = along_y + spready_ref[:, k : k + 1] * stiff_ref[0, k : k + 1, :]
    weight[...] = jnp.dot(along_y, spreadz_ref[...], precision=HIGHEST, preferred_element_type=F32)
    own_hot = (owner_ref[...] == iota((vertices, vertices), 0)).astype(F32).astype(BF16)

    wide = inv_high.shape[2]
    owner_rows = -(-groups // 8) * 8

    def choices(owner, group):
        place = lax.rem(group, per_block) * message + lax.rem(owner, message)
        rows = iota((wide, vertices), 0)
        chosen = jnp.concatenate([rows == c * block + place for c in range(3)], axis=1)
        return chosen.astype(F32).astype(BF16), iota((owner_rows, vertices), 0) == owner // message

    def gradients(own, beyond, to_b, to_z):
        parts = []
        for first in (0, 256):
            columns = [
                jnp.concatenate(
                    [
                        own[c * 4 * ny : (c + 1) * 4 * ny, first : first + 256],
                        beyond[c * ny : (c + 1) * ny, first : first + 256],
                    ],
                    axis=0,
                )
                for c in range(3)
            ]
            parts.append(jnp.concatenate(columns, axis=1))
        to_b[...] = times_left(cross_ref[: 2 * NQ, :], parts[0])
        to_z[...] = times_left(cross_ref[2 * NQ :, :], parts[1])

    def load_change(from_b, from_z, r, half):
        change = []
        for c in range(3):
            s = pl.ds(c * 256 + half * 128, 128)
            change.append(
                [
                    from_b[pl.ds(r, 16), s],
                    from_b[pl.ds(pl.multiple_of(NQ + r, 16), 16), s],
                    from_z[pl.ds(r, 16), s],
                ]
            )
        return change

    pairs = [(0, 0), (1, 1), (2, 2), (0, 1), (0, 2), (1, 2)]

    def fluxes(first):
        def body(i, carry):
            r = pl.multiple_of(i * 16, 16)
            for half in range(2):
                s = pl.ds(half * 128, 128)
                w = weight[pl.ds(r, 16), s]
                if first:
                    grad = load_change(gsb, gsz, r, half)
                    deform = [[grad[c][a] + 1.0 if c == a else grad[c][a] for a in range(3)] for c in range(3)]
                    cg = [sum(deform[k][a] * deform[k][b] for k in range(3)) for a, b in pairs]
                    trace = (0.5 * LAME_FIRST) * (cg[0] + cg[1] + cg[2]) - 1.5 * LAME_FIRST
                    stress = [LAME_SHEAR * t for t in cg]
                    stress = [w * (t - LAME_SHEAR + trace) for t in stress[:3]] + [w * t for t in stress[3:]]
                    for c in range(3):
                        for a in range(3):
                            deform_s[3 * c + a, pl.ds(r, 16), s] = deform[c][a]
                    for k in range(6):
                        stress_s[k, pl.ds(r, 16), s] = stress[k]
                else:
                    deform = [[deform_s[3 * c + a, pl.ds(r, 16), s] for a in range(3)] for c in range(3)]
                    stress = [stress_s[k, pl.ds(r, 16), s] for k in range(6)]
                change = load_change(gvb, gvz, r, half)
                diagonal = [sum(deform[k][a] * change[k][a] for k in range(3)) for a in range(3)]
                trace = LAME_FIRST * (diagonal[0] + diagonal[1] + diagonal[2])
                moved = [w * (2.0 * LAME_SHEAR * t + trace) for t in diagonal]
                shear = LAME_SHEAR * w
                for a, b in pairs[3:]:
                    moved.append(
                        shear * sum(deform[k][a] * change[k][b] + deform[k][b] * change[k][a] for k in range(3))
                    )
                at = [[0, 3, 4], [3, 1, 5], [4, 5, 2]]
                for c in range(3):
                    for a in range(3):
                        entry = sum(change[c][b] * stress[at[b][a]] + deform[c][b] * moved[at[b][a]] for b in range(3))
                        high, low = split(entry)
                        if a < 2:
                            place = pl.ds(pl.multiple_of(c * 2 * NQ + a * NQ + r, 16), 16)
                            fbh[place, s] = high
                            fbl[place, s] = low
                        else:
                            place = pl.ds(pl.multiple_of(c * NQ + r, 16), 16)
                            fzh[place, s] = high
                            fzl[place, s] = low
            return carry

        lax.fori_loop(0, NQ // 16, body, 0)

    def divergence():
        both_b = dot(fbh[...], bzt_ref[...])
        both_z = dot(fzh[...], dzt_ref[...])
        side_b = both_b[:, :lanes] + both_b[:, lanes:] + dot(fbl[...], bzt_ref[:, :lanes])
        side_z = both_z[:, :lanes] + both_z[:, lanes:] + dot(fzl[...], dzt_ref[:, :lanes])
        columns = [
            jnp.concatenate([side_b[c * 2 * NQ : (c + 1) * 2 * NQ], side_z[c * NQ : (c + 1) * NQ]], axis=0)
            for c in range(3)
        ]
        return times_left(crosst_ref[...], jnp.concatenate(columns, axis=1))

    vertex_of_row = lax.rem(iota((48, vertices), 0), 8)
    vertex_mask = vertex_of_row == iota((48, vertices), 1) // count_z

    def restrict(field):
        rows = times_left(hats_ref[...], field)
        rows = jnp.concatenate([rows[:, c * lanes : (c + 1) * lanes] for c in range(3)], axis=0)
        rows = jnp.where(vertex_mask, times_right(rows, hatz_ref[...]), 0.0)
        rows = [jnp.sum(rows[8 * i : 8 * i + 8], axis=0, keepdims=True) for i in range(6)]
        fill = jnp.zeros((5, vertices), F32)
        return (
            jnp.concatenate([rows[0], rows[2], rows[4], fill], axis=0),
            jnp.concatenate([rows[1], rows[3], rows[5], fill], axis=0),
        )

    def widened(own, beyond):
        return jnp.concatenate([jnp.concatenate([own[c], beyond[c]], axis=0) for c in range(3)], axis=1)

    loaded(2, 9, 10, 11, 12, 13)
    own_rhs = [rhs_ref[c].reshape(4 * ny, lanes) for c in range(3)]

    @pl.when(jnp.logical_not(is_last))
    def _():
        halo[0].wait_recv()

    beyond_state = [jnp.where(is_last, 0.0, halo_state[c]) for c in range(3)]
    gradients(state_z, along_z(beyond_state), gsb, gsz)

    @pl.when(jnp.logical_not(is_last))
    def _():
        for copy in halo[1:]:
            copy.wait_recv()

    keep_right = jnp.where(is_last, 0.0, keep_of(clamp_column(halo_clamp, 0)))
    beyond_direction = [jnp.where(is_last, 0.0, keep_right * halo_rx[c]) for c in range(3)]
    owner_right = halo_owner[...]
    right_hot = (owner_right == iota((vertices, vertices), 0)).astype(F32).astype(BF16)
    gradients(direction_z, along_z(beyond_direction), gvb, gvz)
    fluxes(True)
    image = divergence()

    def settle(image, field):
        own, beyond = [], []
        for c in range(3):
            part = image[:, c * lanes : (c + 1) * lanes]
            own.append(own_rhs[c] - keep * part[: 4 * ny] - (1.0 - keep) * field[c])
            beyond.append(-keep_right * part[4 * ny :])
        return own, beyond

    own_first, beyond_first = settle(image, own_direction)
    low_sums, high_sums = restrict(widened(own_first, beyond_first))
    high_sums = jnp.where(is_last, 0.0, high_sums)
    sums_tx[0] = stacked_exact(low_sums, own_hot, dot_nt)
    sums_tx[1] = stacked_exact(high_sums, right_hot, dot_nt)

    def send_own(d):
        p = lax.rem(g + d, groups)
        remote(
            sums_tx.at[0, pl.ds(0, 4)], sums_rx.at[g, pl.ds(0, 4)], sums_send.at[d], sums_recv.at[g], (p, m)
        ).start()

    def send_next(d):
        p = lax.rem(g_right + d, groups)
        remote(
            sums_tx.at[1, pl.ds(0, 4)],
            sums_rx.at[groups + g_right, pl.ds(0, 4)],
            sums_send.at[groups + d],
            sums_recv.at[groups + g_right],
            (p, m_right),
        ).start()

    @pl.when(jnp.logical_not(is_last))
    def _():
        each(0, groups, send_next)

    each(1, groups, send_own)
    sums_rx[g] = sums_tx[0]

    @pl.when(at_start)
    def _():
        sums_rx[groups] = jnp.zeros((8, vertices), F32)

    loaded(6)
    inv_high[...] = jnp.zeros_like(inv_high)
    inv_low[...] = jnp.zeros_like(inv_low)
    for b in range(blocks):
        high, low = split(inverse_ref[0, b])
        inv_high[b, :size, :size] = high
        inv_low[b, :size, :size] = low
    pick = (
        iota((vertices, wide), 0) == g * message + lax.rem(iota((vertices, wide), 1), message)
    ).astype(F32).astype(BF16)
    shape = (groups * 8, wide)
    row, lane = iota(shape, 0), iota(shape, 1)
    pick_mask = (
        (lane // block == lax.rem(row, 8))
        & (lax.rem(lane, block) // message == lax.rem(row // 8, per_block))
        & (lane < size)
    )

    def got_own(d):
        p = lax.rem(g + d, groups)
        remote(
            sums_tx.at[0, pl.ds(0, 4)], sums_rx.at[p, pl.ds(0, 4)], sums_send.at[d], sums_recv.at[p], (p, m)
        ).wait()

    def next_copy(p):
        return remote(
            sums_tx.at[1, pl.ds(0, 4)],
            sums_rx.at[groups + p, pl.ds(0, 4)],
            sums_send.at[groups + p],
            sums_recv.at[groups + p],
            right,
        )

    def got_next(p):
        @pl.when(jnp.logical_not(at_start & (p == 0)))
        def _():
            next_copy(p).wait_recv()

    each(1, groups, got_own)
    each(0, groups, got_next)

    received = sums_rx[:groups] + sums_rx[groups:]
    received = received.reshape(groups * 8, vertices)
    placed = jnp.where(pick_mask, stacked_exact(received, pick, dot), 0.0)
    vectors = [
        jnp.sum(placed[b * per_block * 8 : (b + 1) * per_block * 8], axis=0, keepdims=True) for b in range(blocks)
    ]
    for b in range(blocks):
        high, low = split(jnp.broadcast_to(vectors[b], (8, wide)))
        both = dot_nt(jnp.concatenate([high, low], axis=0), inv_high[b])
        solved_tx[b] = (both[:1] + both[8:9]) + dot_nt(jnp.concatenate([high, high], axis=0), inv_low[b])[:1]

    def return_own(d):
        p = lax.rem(g + d, groups)
        remote(
            solved_tx.at[p // per_block], solved_rx.at[g], solved_send.at[d], solved_recv.at[g], (p, m)
        ).start()

    def left_copy(d):
        p = lax.rem(g + d, groups)
        before = lax.rem(p + groups - at_start.astype(jnp.int32), groups)
        return p, remote(
            solved_tx.at[p // per_block],
            solved_rx.at[groups + g],
            solved_send.at[groups + d],
            solved_recv.at[groups + g],
            (before, m_left),
        )

    def return_left(d):
        p, copy = left_copy(d)
        pl.when(jnp.logical_not(at_start & (p == 0)))(copy.start)

    def left_sent(d):
        p, copy = left_copy(d)
        pl.when(jnp.logical_not(at_start & (p == 0)))(copy.wait_send)

    each(0, groups, return_left)
    each(1, groups, return_own)
    solved_rx[g] = solved_tx[g // per_block]
    loaded(14, 15)
    own_choices = choices(owner_ref[...], g)
    right_choices = choices(owner_right, g_right)

    def back_own(d):
        p = lax.rem(g + d, groups)
        remote(solved_tx.at[0], solved_rx.at[p], solved_send.at[d], solved_recv.at[p], (p, m)).wait()

    def back_next(p):
        remote(
            solved_tx.at[0], solved_rx.at[groups + p], solved_send.at[groups + p], solved_recv.at[groups + p], right
        ).wait_recv()

    each(1, groups, back_own)

    @pl.when(jnp.logical_not(is_last))
    def _():
        each(0, groups, back_next)


    def corrections(start, chosen, mask):
        at_row = iota((owner_rows, wide), 0)
        gathered = jnp.zeros((owner_rows, wide), F32)
        for p in range(groups):
            gathered = jnp.where(at_row == p, jnp.broadcast_to(solved_rx[start + p], gathered.shape), gathered)
        values = stacked_exact(gathered, chosen, dot)
        values = [values[:, c * vertices : (c + 1) * vertices] for c in range(3)]
        return [jnp.sum(jnp.where(mask, t, 0.0), axis=0, keepdims=True) for t in values]

    own_correction = corrections(0, *own_choices)
    next_correction = [jnp.where(is_last, 0.0, t) for t in corrections(groups, *right_choices)]
    rows = []
    for c in range(3):
        rows.append(jnp.broadcast_to(own_correction[c], (8, vertices)))
        rows.append(jnp.broadcast_to(next_correction[c], (8, vertices)))
    rows = jnp.where(vertex_mask, jnp.concatenate(rows, axis=0), 0.0)
    rows = times_right(rows, hatzp_ref[...])
    rows = jnp.concatenate([rows[16 * c : 16 * c + 16] for c in range(3)], axis=1)
    update = times_left(hatst_ref[...], rows)
    new_direction, beyond_new = [], []
    for c in range(3):
        part = update[:, c * lanes : (c + 1) * lanes]
        new_direction.append(own_direction[c] + keep * part[: 4 * ny])
        beyond_new.append(beyond_direction[c] + keep_right * part[4 * ny :])
        new_ref[c] = new_direction[c].reshape(4, ny, lanes)
    store_new = pltpu.make_async_copy(new_ref, outputs[0], store_sem.at[0])
    store_new.start()
    beyond_new = [jnp.where(is_last, 0.0, t) for t in beyond_new]
    gradients(along_z([keep * t for t in new_direction]), along_z(beyond_new), gvb, gvz)
    fluxes(False)
    image = divergence()
    for c in range(3):
        last_tx[c * ny : (c + 1) * ny, :] = image[4 * ny :, c * lanes : (c + 1) * lanes]
    copy_layer = remote(
        last_tx.at[pl.ds(0, 3 * ny)], last_rx.at[pl.ds(0, 3 * ny)], last_send.at[0], last_recv.at[0], right
    )
    pl.when(jnp.logical_not(is_last))(copy_layer.start)
    own_last, beyond_last = settle(image, new_direction)
    low_sums, high_sums = restrict(widened(own_last, beyond_last))
    last_tx[3 * ny :, :] = high_sums
    copy_sums = remote(
        last_tx.at[pl.ds(3 * ny, 8)], last_rx.at[pl.ds(3 * ny, 8)], last_send.at[1], last_recv.at[1], right
    )
    pl.when(jnp.logical_not(is_last))(copy_sums.start)
    for c in range(3):
        residual_ref[c, 1:] = own_last[c][ny:].reshape(3, ny, lanes)
    store_rest = pltpu.make_async_copy(residual_ref.at[:, 1:], outputs[1].at[:, 1:], store_sem.at[1])
    store_rest.start()
    pl.when(jnp.logical_not(is_first))(copy_layer.wait_recv)
    for c in range(3):
        arrived = jnp.where(is_first, 0.0, last_rx[c * ny : (c + 1) * ny, :])
        residual_ref[c, 0] = own_last[c][:ny] - keep[:ny] * arrived
    store_first = pltpu.make_async_copy(residual_ref.at[:, 0], outputs[1].at[:, 0], store_sem.at[2])
    store_first.start()
    pl.when(jnp.logical_not(is_first))(copy_sums.wait_recv)
    total = low_sums + jnp.where(is_first, 0.0, last_rx[3 * ny :, :])
    for c in range(3):
        for k in range(count_y):
            coarse_ref[c, 0, k : k + 1, :] = total[c : c + 1, k * count_z : (k + 1) * count_z]
    store_coarse = pltpu.make_async_copy(coarse_ref, outputs[2], store_sem.at[3])
    store_coarse.start()
    each(0, groups, left_sent)

    @pl.when(jnp.logical_not(is_first))
    def _():
        for copy in halo:
            copy.wait_send()

    @pl.when(jnp.logical_not(is_last))
    def _():
        each(0, groups, lambda p: next_copy(p).wait_send())
        copy_layer.wait_send()
        copy_sums.wait_send()

    for copy in (store_new, store_rest, store_first, store_coarse):
        copy.wait()


def write_out(*refs):
    sources, targets, held, sems = refs[:3], refs[3:6], refs[6:9], refs[9]
    loads = [pltpu.make_async_copy(a, b, sems.at[i]) for i, (a, b) in enumerate(zip(sources, held))]
    stores = [pltpu.make_async_copy(a, b, sems.at[3 + i]) for i, (a, b) in enumerate(zip(held, targets))]
    for copy in loads:
        copy.start()
    for load, store in zip(loads, stores):
        load.wait()
        store.start()
    for copy in stores:
        copy.wait()


def shards(groups, members, state, direction, rhs, clamp, stiffness, coarse_owner, coarse_inverse):
    count_y, count_z = stiffness.shape[1:]
    ny, nz = 4 * count_y, 4 * count_z
    tables = [jnp.asarray(t.astype(np.float32)) for t in constant_tables(count_y, count_z)]
    blocks, size = coarse_inverse.shape[1:3]
    wide = -(-size // 128) * 128
    vertices = count_y * count_z
    results = tuple(
        jax.ShapeDtypeStruct(t, F32) for t in (state.shape, state.shape, (3, 1, count_y, count_z))
    )
    operands = [state, direction, rhs, clamp, stiffness, coarse_owner, coarse_inverse, *tables]
    new, residual, coarse = pl.pallas_call(
        functools.partial(kernel, groups, members),
        out_shape=results,
        in_specs=[pl.BlockSpec(memory_space=pl.ANY)] * INPUTS,
        out_specs=[pl.BlockSpec(memory_space=pl.ANY)] * 3,
        scratch_shapes=[pltpu.VMEM(t.shape, t.dtype) for t in operands]
        + [pltpu.VMEM(t.shape, F32) for t in results]
        + [pltpu.VMEM(t.shape, BF16) for t in tables[:9]]
        + [
            pltpu.VMEM(clamp.shape, jnp.int32),
            pltpu.VMEM(coarse_owner.shape, jnp.int32),
            pltpu.VMEM((3, ny, nz), F32),
            pltpu.VMEM((3, ny, nz), F32),
            pltpu.VMEM((2, 8, vertices), F32),
            pltpu.VMEM((2 * groups, 8, vertices), F32),
            pltpu.VMEM((blocks, 1, wide), F32),
            pltpu.VMEM((2 * groups, 1, wide), F32),
            pltpu.VMEM((3 * ny + 8, nz), F32),
            pltpu.VMEM((3 * ny + 8, nz), F32),
            pltpu.VMEM((blocks, wide, wide), BF16),
            pltpu.VMEM((blocks, wide, wide), BF16),
            pltpu.VMEM((NQ, 256), F32),
            pltpu.VMEM((2 * NQ, 768), F32),
            pltpu.VMEM((NQ, 768), F32),
            pltpu.VMEM((2 * NQ, 768), F32),
            pltpu.VMEM((NQ, 768), F32),
            pltpu.VMEM((9, NQ, 256), F32),
            pltpu.VMEM((6, NQ, 256), F32),
            pltpu.VMEM((6 * NQ, 256), BF16),
            pltpu.VMEM((6 * NQ, 256), BF16),
            pltpu.VMEM((3 * NQ, 256), BF16),
            pltpu.VMEM((3 * NQ, 256), BF16),
            pltpu.SemaphoreType.DMA((4,)),
            pltpu.SemaphoreType.DMA((4,)),
            pltpu.SemaphoreType.DMA((2 * groups,)),
            pltpu.SemaphoreType.DMA((2 * groups,)),
            pltpu.SemaphoreType.DMA((2 * groups,)),
            pltpu.SemaphoreType.DMA((2 * groups,)),
            pltpu.SemaphoreType.DMA((2,)),
            pltpu.SemaphoreType.DMA((2,)),
            pltpu.SemaphoreType.DMA((INPUTS,)),
            pltpu.SemaphoreType.DMA((4,)),
        ],
        compiler_params=pltpu.CompilerParams(
            collective_id=0, has_side_effects=True, vmem_limit_bytes=56 * 1024 * 1024
        ),
    )(*operands)
    return pl.pallas_call(
        write_out,
        out_shape=results,
        in_specs=[pl.BlockSpec(memory_space=pl.ANY)] * 3,
        out_specs=[pl.BlockSpec(memory_space=pl.ANY)] * 3,
        scratch_shapes=[pltpu.VMEM(t.shape, F32) for t in results] + [pltpu.SemaphoreType.DMA((6,))],
        compiler_params=pltpu.CompilerParams(vmem_limit_bytes=56 * 1024 * 1024),
    )(new, residual, coarse)


def solution(mesh):
    in_specs = (
        P(None, ("grp", "mem"), None, None),
        P(None, ("grp", "mem"), None, None),
        P(None, ("grp", "mem"), None, None),
        P(("grp", "mem"), None),
        P(("grp", "mem"), None, None),
        P(("grp", "mem"), None),
        P(("grp", "mem"), None, None, None),
    )
    out_specs = (
        P(None, ("grp", "mem"), None, None),
        P(None, ("grp", "mem"), None, None),
        P(None, ("grp", "mem"), None, None),
    )
    body = functools.partial(shards, mesh.shape["grp"], mesh.shape["mem"])
    return jax.shard_map(body, mesh=mesh, in_specs=in_specs, out_specs=out_specs, check_vma=False)
```

```python
import functools

import jax
import jax.numpy as jnp
import ml_dtypes
import numpy as np
from jax import lax
from jax.experimental import pallas as pl
from jax.experimental.pallas import tpu as pltpu
from jax.sharding import PartitionSpec as P

LAME_FIRST = 1.2
LAME_SHEAR = 0.8
HIGHEST = lax.Precision.HIGHEST
MESH = pl.DeviceIdType.MESH
F32 = jnp.float32
BF16 = jnp.bfloat16
INPUTS = 18
NQ = 112


def gauss_rule():
    inner = np.sqrt(5.0 - 2.0 * np.sqrt(10.0 / 7.0)) / 3.0
    outer = np.sqrt(5.0 + 2.0 * np.sqrt(10.0 / 7.0)) / 3.0
    inner_weight = (322.0 + 13.0 * np.sqrt(70.0)) / 900.0
    outer_weight = (322.0 - 13.0 * np.sqrt(70.0)) / 900.0
    points = np.array([-outer, -inner, 0.0, inner, outer])
    weights = np.array([outer_weight, inner_weight, 128.0 / 225.0, inner_weight, outer_weight])
    return (points, weights)


def basis_tables():
    gll_points = np.array([-1.0, -np.sqrt(3.0 / 7.0), 0.0, np.sqrt(3.0 / 7.0), 1.0])
    gauss_points, gauss_weights = gauss_rule()
    values = np.zeros((5, 5))
    slopes = np.zeros((5, 5))
    for j in range(5):
        others = [gll_points[k] for k in range(5) if k != j]
        denominator = np.prod([gll_points[j] - o for o in others])
        for q in range(5):
            t = gauss_points[q]
            values[q, j] = np.prod([t - o for o in others]) / denominator
            total = 0.0
            for i in range(4):
                total += np.prod([t - others[k] for k in range(4) if k != i])
            slopes[q, j] = 2.0 * total / denominator
    return (gll_points, gauss_weights, values, slopes)


def banded(table, count):
    banded_matrix = np.zeros((5 * count, 4 * count + 1))
    for e in range(count):
        banded_matrix[5 * e : 5 * e + 5, 4 * e : 4 * e + 5] = table
    return banded_matrix[:, :-1]


def restrictor(gll_points, count):
    result = np.zeros((count, 4 * count))
    for e in range(count):
        for j in range(4):
            result[e, 4 * e + j] += (1.0 - gll_points[j]) / 2.0
            if e + 1 < count:
                result[e + 1, 4 * e + j] += (1.0 + gll_points[j]) / 2.0
    return result


def halves(table):
    high = table.astype(ml_dtypes.bfloat16)
    low = (table - high.astype(np.float64)).astype(ml_dtypes.bfloat16)
    return high, low


def padded(table, axis, multiple):
    widths = [(0, 0), (0, 0)]
    widths[axis] = (0, -table.shape[axis] % multiple)
    return np.pad(table, widths)


def left_table(table):
    high, low = halves(table)
    return padded(np.concatenate([high, high, low], axis=1), 1, 128)


def constant_tables(count_y, count_z):
    gll_points, weights, values, slopes = basis_tables()
    by, dy = banded(values, count_y), banded(slopes, count_y)
    bz, dz = banded(values, count_z), banded(slopes, count_z)
    pads = lambda t: np.pad(t, ((0, NQ - t.shape[0]), (0, 0)))
    cross = np.concatenate(
        [pads(np.kron(slopes, by)), pads(np.kron(values, dy)), pads(np.kron(values, by))]
    )
    bz, dz = padded(bz, 0, 256), padded(dz, 0, 256)
    low_hat = np.append((1.0 - gll_points[:4]) / 2.0, 0.0)
    high_hat = np.append((1.0 + gll_points[:4]) / 2.0, 1.0)
    hat_y = restrictor(gll_points, count_y)
    hat_z = restrictor(gll_points, count_z)
    hats = np.zeros((16, 20 * count_y))
    hats[:count_y] = np.kron(low_hat[None], hat_y)
    hats[8 : 8 + count_y] = np.kron(high_hat[None], hat_y)
    tiled = np.tile(hat_z, (count_y, 1))
    spread_y = np.zeros((NQ, count_y))
    spread_y[:100] = np.kron(weights[:, None], np.kron(np.eye(count_y), weights[:, None])) / 8.0
    spread_z = padded(np.kron(np.eye(count_z), weights[None]), 1, 256)
    return (
        left_table(cross),
        np.concatenate([bz.T, dz.T], axis=1),
        bz,
        dz,
        left_table(cross.T),
        left_table(hats),
        tiled.T,
        tiled,
        left_table(hats.T),
        spread_y.astype(np.float32),
        spread_z.astype(np.float32),
    )


def split(x):
    high = x.astype(BF16)
    return high, (x - high.astype(F32)).astype(BF16)


def dot(a, b):
    return lax.dot_general(a, b, (((1,), (0,)), ((), ())), preferred_element_type=F32)


def dot_nt(a, b):
    return lax.dot_general(a, b, (((1,), (1,)), ((), ())), preferred_element_type=F32)


def times_right(x, table):
    high, low = split(x)
    return dot(jnp.concatenate([high, low, high], axis=1), table)


def times_left(table, x):
    high, low = split(x)
    parts = [high, low, high]
    rest = table.shape[1] - 3 * x.shape[0]
    if rest:
        parts.append(jnp.zeros((rest, x.shape[1]), BF16))
    return dot(table, jnp.concatenate(parts, axis=0))


def stacked_exact(x, one_hot, product):
    rows = x.shape[0]
    high, low = split(x)
    both = product(jnp.concatenate([high, low], axis=0), one_hot)
    return both[:rows] + both[rows:]


def iota(shape, axis):
    return lax.broadcasted_iota(jnp.int32, shape, axis)


def each(low, high, act):
    if high - low <= 8:
        for i in range(low, high):
            act(i)
    else:

        def step(i, carry):
            act(i)
            return carry

        lax.fori_loop(low, high, step, 0)


def kernel(groups, members, *refs):
    sources, outputs = refs[:INPUTS], refs[INPUTS : INPUTS + 3]
    local, scratch = refs[INPUTS + 3 : 2 * INPUTS + 3], refs[2 * INPUTS + 3 :]
    state_ref, direction_ref, rhs_ref, clamp_ref, stiff_ref, owner_ref, inverse_ref = local[:7]
    spready_ref, spreadz_ref = local[16:]
    new_ref, residual_ref, coarse_ref = scratch[:3]
    narrow = scratch[3:12]
    cross_ref, bdz_ref, bzt_ref, dzt_ref, crosst_ref, hats_ref, hatz_ref, hatzp_ref, hatst_ref = narrow
    (
        halo_clamp,
        halo_owner,
        halo_state,
        halo_rx,
        sums_tx,
        sums_rx,
        solved_tx,
        solved_rx,
        last_tx,
        last_rx,
        inv_high,
        inv_low,
        weight,
        gsb,
        gsz,
        gvb,
        gvz,
        deform_s,
        stress_s,
        fbh,
        fbl,
        fzh,
        fzl,
        halo_send,
        halo_recv,
        sums_send,
        sums_recv,
        solved_send,
        solved_recv,
        last_send,
        last_recv,
        load_sem,
        store_sem,
    ) = scratch[12:]
    count_y, count_z = stiff_ref.shape[1:]
    ny = 4 * count_y
    vertices = count_y * count_z
    blocks = inverse_ref.shape[1]
    size = inverse_ref.shape[2]
    block = size // 3
    message = vertices // groups
    per_block = groups // blocks
    g = lax.axis_index("grp")
    m = lax.axis_index("mem")
    m_right = lax.rem(m + 1, members)
    m_left = lax.rem(m + members - 1, members)
    at_end = m == members - 1
    at_start = m == 0
    g_right = lax.rem(g + at_end.astype(jnp.int32), groups)
    g_left = lax.rem(g + groups - at_start.astype(jnp.int32), groups)
    is_last = (g * members + m) == groups * members - 1
    is_first = (g * members + m) == 0

    barrier = pltpu.get_barrier_semaphore()

    def greet(p, member):
        pl.semaphore_signal(barrier, inc=1, device_id=(p, member), device_id_type=MESH)

    greet(g_left, m_left)
    each(1, groups, lambda d: greet(lax.rem(g_left + d, groups), m_left))
    each(0, groups, lambda d: greet(lax.rem(g_right + d, groups), m_right))
    each(1, groups, lambda d: greet(lax.rem(g + d, groups), m))
    loads = [pltpu.make_async_copy(a, b, load_sem.at[i]) for i, (a, b) in enumerate(zip(sources, local))]
    order = [3, 5, 1, 0, 8, 4, 16, 17, 7, 9, 10, 11, 2, 12, 13, 6]
    for i in order + [i for i in range(INPUTS) if i not in order]:
        loads[i].start()

    def loaded(*which):
        for i in which:
            loads[i].wait()
            if 7 <= i < 16:
                target = narrow[i - 7]
                rows, columns = local[i].shape
                if target.shape == local[i].shape:
                    target[...] = local[i][...].astype(BF16)
                    continue
                high, low = split(local[i][...])
                target[:rows, :columns] = high
                if target.shape[0] == rows:
                    target[:, columns:] = low
                else:
                    target[rows : 2 * rows, :] = high
                    target[2 * rows :, :] = low

    pl.semaphore_wait(barrier, 3 * groups - 1)

    def along_z(parts):
        return times_right(jnp.concatenate(parts, axis=0), bdz_ref[...])

    left = (g_left, m_left)
    right = (g_right, m_right)

    def remote(src, dst, send, recv, device):
        return pltpu.make_async_remote_copy(
            src_ref=src, dst_ref=dst, send_sem=send, recv_sem=recv, device_id=device, device_id_type=MESH
        )

    halo = [
        remote(a, b, halo_send.at[i], halo_recv.at[i], left)
        for i, (a, b) in enumerate(
            (
                (sources[0].at[:, 0], halo_state),
                (sources[1].at[:, 0], halo_rx),
                (sources[3], halo_clamp),
                (sources[5], halo_owner),
            )
        )
    ]

    @pl.when(jnp.logical_not(is_first))
    def _():
        for copy in halo:
            copy.start()

    def clamp_column(ref, x):
        row = jnp.broadcast_to(ref[x : x + 1, :].astype(F32), (ny, ny))
        return jnp.sum(jnp.where(iota((ny, ny), 0) == iota((ny, ny), 1), row, 0.0), axis=1, keepdims=True)

    def keep_of(column):
        shape = (column.shape[0], lanes)
        return jnp.where(iota(shape, 1) == 0, jnp.broadcast_to(1.0 - column, shape), 1.0)

    lanes = 4 * count_z
    loaded(3, 5, 1)
    keep = keep_of(jnp.concatenate([clamp_column(clamp_ref, x) for x in range(4)], axis=0))

    loaded(0, 8)
    own_state = [state_ref[c].reshape(4 * ny, lanes) for c in range(3)]
    own_direction = [direction_ref[c].reshape(4 * ny, lanes) for c in range(3)]
    own_z = along_z(own_state + [keep * t for t in own_direction])
    sums_rx[:, 4:, :] = jnp.zeros((2 * groups, 4, vertices), F32)
    loaded(4, 16, 17, 7)
    along_y = jnp.zeros((NQ, count_z), F32)
    for k in range(count_y):
        along_y = along_y + spready_ref[:, k : k + 1] * stiff_ref[0, k : k + 1, :]
    weight[...] = jnp.dot(along_y, spreadz_ref[...], precision=HIGHEST, preferred_element_type=F32)
    own_hot = (owner_ref[...] == iota((vertices, vertices), 0)).astype(F32).astype(BF16)

    wide = inv_high.shape[2]
    owner_rows = -(-groups // 8) * 8

    def choices(owner, group):
        place = lax.rem(group, per_block) * message + lax.rem(owner, message)
        rows = iota((wide, vertices), 0)
        chosen = jnp.concatenate([rows == c * block + place for c in range(3)], axis=1)
        return chosen.astype(F32).astype(BF16), iota((owner_rows, vertices), 0) == owner // message

    def gradients(columns, targets):
        for first, rows, place in ((0, pl.ds(0, 2 * NQ), 0), (256, pl.ds(2 * NQ, NQ), 1)):
            wide_field = jnp.concatenate([t[:, first : first + 256] for t in columns], axis=1)
            result = times_left(cross_ref[rows, :], wide_field)
            for i, target in enumerate(targets):
                target[place][...] = result[:, i * 768 : (i + 1) * 768]

    def load_change(from_b, from_z, r, half):
        change = []
        for c in range(3):
            s = pl.ds(c * 256 + half * 128, 128)
            change.append(
                [
                    from_b[pl.ds(r, 16), s],
                    from_b[pl.ds(pl.multiple_of(NQ + r, 16), 16), s],
                    from_z[pl.ds(r, 16), s],
                ]
            )
        return change

    pairs = [(0, 0), (1, 1), (2, 2), (0, 1), (0, 2), (1, 2)]

    def fluxes(first):
        def body(i, carry):
            r = pl.multiple_of(i * 16, 16)
            for half in range(2):
                s = pl.ds(half * 128, 128)
                w = weight[pl.ds(r, 16), s]
                if first:
                    grad = load_change(gsb, gsz, r, half)
                    deform = [[grad[c][a] + 1.0 if c == a else grad[c][a] for a in range(3)] for c in range(3)]
                    cg = [sum(deform[k][a] * deform[k][b] for k in range(3)) for a, b in pairs]
                    trace = (0.5 * LAME_FIRST) * (cg[0] + cg[1] + cg[2]) - 1.5 * LAME_FIRST
                    stress = [LAME_SHEAR * t for t in cg]
                    stress = [w * (t - LAME_SHEAR + trace) for t in stress[:3]] + [w * t for t in stress[3:]]
                    for c in range(3):
                        for a in range(3):
                            deform_s[3 * c + a, pl.ds(r, 16), s] = deform[c][a]
                    for k in range(6):
                        stress_s[k, pl.ds(r, 16), s] = stress[k]
                else:
                    deform = [[deform_s[3 * c + a, pl.ds(r, 16), s] for a in range(3)] for c in range(3)]
                    stress = [stress_s[k, pl.ds(r, 16), s] for k in range(6)]
                change = load_change(gvb, gvz, r, half)
                diagonal = [sum(deform[k][a] * change[k][a] for k in range(3)) for a in range(3)]
                trace = LAME_FIRST * (diagonal[0] + diagonal[1] + diagonal[2])
                moved = [w * (2.0 * LAME_SHEAR * t + trace) for t in diagonal]
                shear = LAME_SHEAR * w
                for a, b in pairs[3:]:
                    moved.append(
                        shear * sum(deform[k][a] * change[k][b] + deform[k][b] * change[k][a] for k in range(3))
                    )
                at = [[0, 3, 4], [3, 1, 5], [4, 5, 2]]
                for c in range(3):
                    for a in range(3):
                        entry = sum(change[c][b] * stress[at[b][a]] + deform[c][b] * moved[at[b][a]] for b in range(3))
                        high, low = split(entry)
                        if a < 2:
                            place = pl.ds(pl.multiple_of(c * 2 * NQ + a * NQ + r, 16), 16)
                            fbh[place, s] = high
                            fbl[place, s] = low
                        else:
                            place = pl.ds(pl.multiple_of(c * NQ + r, 16), 16)
                            fzh[place, s] = high
                            fzl[place, s] = low
            return carry

        lax.fori_loop(0, NQ // 16, body, 0)

    def divergence():
        both_b = dot(fbh[...], bzt_ref[...])
        both_z = dot(fzh[...], dzt_ref[...])
        side_b = both_b[:, :lanes] + both_b[:, lanes:] + dot(fbl[...], bzt_ref[:, :lanes])
        side_z = both_z[:, :lanes] + both_z[:, lanes:] + dot(fzl[...], dzt_ref[:, :lanes])
        columns = [
            jnp.concatenate([side_b[c * 2 * NQ : (c + 1) * 2 * NQ], side_z[c * NQ : (c + 1) * NQ]], axis=0)
            for c in range(3)
        ]
        return times_left(crosst_ref[...], jnp.concatenate(columns, axis=1))

    vertex_of_row = lax.rem(iota((48, vertices), 0), 8)
    vertex_mask = vertex_of_row == iota((48, vertices), 1) // count_z

    def restrict(field):
        rows = times_left(hats_ref[...], field)
        rows = jnp.concatenate([rows[:, c * lanes : (c + 1) * lanes] for c in range(3)], axis=0)
        rows = jnp.where(vertex_mask, times_right(rows, hatz_ref[...]), 0.0)
        rows = [jnp.sum(rows[8 * i : 8 * i + 8], axis=0, keepdims=True) for i in range(6)]
        fill = jnp.zeros((5, vertices), F32)
        return (
            jnp.concatenate([rows[0], rows[2], rows[4], fill], axis=0),
            jnp.concatenate([rows[1], rows[3], rows[5], fill], axis=0),
        )

    def widened(own, beyond):
        return jnp.concatenate([jnp.concatenate([own[c], beyond[c]], axis=0) for c in range(3)], axis=1)

    loaded(2, 9, 10, 11, 12, 13)
    own_rhs = [rhs_ref[c].reshape(4 * ny, lanes) for c in range(3)]

    @pl.when(jnp.logical_not(is_last))
    def _():
        for copy in halo:
            copy.wait_recv()

    beyond_state = [jnp.where(is_last, 0.0, halo_state[c]) for c in range(3)]
    keep_right = jnp.where(is_last, 0.0, keep_of(clamp_column(halo_clamp, 0)))
    beyond_direction = [jnp.where(is_last, 0.0, keep_right * halo_rx[c]) for c in range(3)]
    owner_right = halo_owner[...]
    right_hot = (owner_right == iota((vertices, vertices), 0)).astype(F32).astype(BF16)
    beyond_z = along_z(beyond_state + beyond_direction)
    columns = [
        jnp.concatenate([own_z[i * 4 * ny : (i + 1) * 4 * ny], beyond_z[i * ny : (i + 1) * ny]], axis=0)
        for i in range(6)
    ]
    gradients(columns, ((gsb, gsz), (gvb, gvz)))
    fluxes(True)
    image = divergence()

    def settle(image, field):
        own, beyond = [], []
        for c in range(3):
            part = image[:, c * lanes : (c + 1) * lanes]
            own.append(own_rhs[c] - keep * part[: 4 * ny] - (1.0 - keep) * field[c])
            beyond.append(-keep_right * part[4 * ny :])
        return own, beyond

    own_first, beyond_first = settle(image, own_direction)
    low_sums, high_sums = restrict(widened(own_first, beyond_first))
    high_sums = jnp.where(is_last, 0.0, high_sums)
    sums_tx[0] = stacked_exact(low_sums, own_hot, dot_nt)
    sums_tx[1] = stacked_exact(high_sums, right_hot, dot_nt)

    def far(i):
        return jnp.where(g >= groups // 2, i, groups - 1 - i)

    def send_own(i):
        p = far(i)

        @pl.when(p != g)
        def _():
            remote(
                sums_tx.at[0, pl.ds(0, 4)], sums_rx.at[g, pl.ds(0, 4)], sums_send.at[p], sums_recv.at[g], (p, m)
            ).start()

    def send_next(i):
        p = far(i)
        remote(
            sums_tx.at[1, pl.ds(0, 4)],
            sums_rx.at[groups + g_right, pl.ds(0, 4)],
            sums_send.at[groups + p],
            sums_recv.at[groups + g_right],
            (p, m_right),
        ).start()

    @pl.when(jnp.logical_not(is_last))
    def _():
        each(0, groups, send_next)

    each(0, groups, send_own)
    sums_rx[g] = sums_tx[0]

    @pl.when(at_start)
    def _():
        sums_rx[groups] = jnp.zeros((8, vertices), F32)

    loaded(6)
    inv_high[...] = jnp.zeros_like(inv_high)
    inv_low[...] = jnp.zeros_like(inv_low)
    for b in range(blocks):
        high, low = split(inverse_ref[0, b])
        inv_high[b, :size, :size] = high
        inv_low[b, :size, :size] = low
    pick = (
        iota((vertices, wide), 0) == g * message + lax.rem(iota((vertices, wide), 1), message)
    ).astype(F32).astype(BF16)
    shape = (groups * 8, wide)
    row, lane = iota(shape, 0), iota(shape, 1)
    pick_mask = (
        (lane // block == lax.rem(row, 8))
        & (lax.rem(lane, block) // message == lax.rem(row // 8, per_block))
        & (lane < size)
    )

    def got_own(d):
        p = lax.rem(g + d, groups)
        remote(
            sums_tx.at[0, pl.ds(0, 4)], sums_rx.at[p, pl.ds(0, 4)], sums_send.at[p], sums_recv.at[p], (p, m)
        ).wait()

    def next_copy(p):
        return remote(
            sums_tx.at[1, pl.ds(0, 4)],
            sums_rx.at[groups + p, pl.ds(0, 4)],
            sums_send.at[groups + p],
            sums_recv.at[groups + p],
            right,
        )

    def got_next(p):
        @pl.when(jnp.logical_not(at_start & (p == 0)))
        def _():
            next_copy(p).wait_recv()

    each(1, groups, got_own)
    each(0, groups, got_next)

    received = sums_rx[:groups] + sums_rx[groups:]
    received = received.reshape(groups * 8, vertices)
    placed = jnp.where(pick_mask, stacked_exact(received, pick, dot), 0.0)
    vectors = [
        jnp.sum(placed[b * per_block * 8 : (b + 1) * per_block * 8], axis=0, keepdims=True) for b in range(blocks)
    ]
    for b in range(blocks):
        high, low = split(jnp.broadcast_to(vectors[b], (8, wide)))
        both = dot_nt(jnp.concatenate([high, low], axis=0), inv_high[b])
        solved_tx[b] = (both[:1] + both[8:9]) + dot_nt(jnp.concatenate([high, high], axis=0), inv_low[b])[:1]

    def return_own(i):
        p = far(i)

        @pl.when(p != g)
        def _():
            remote(
                solved_tx.at[p // per_block], solved_rx.at[g], solved_send.at[p], solved_recv.at[g], (p, m)
            ).start()

    def left_copy(i):
        p = far(i)
        before = lax.rem(p + groups - at_start.astype(jnp.int32), groups)
        return p, remote(
            solved_tx.at[p // per_block],
            solved_rx.at[groups + g],
            solved_send.at[groups + p],
            solved_recv.at[groups + g],
            (before, m_left),
        )

    def return_left(d):
        p, copy = left_copy(d)
        pl.when(jnp.logical_not(at_start & (p == 0)))(copy.start)

    def left_sent(d):
        p, copy = left_copy(d)
        pl.when(jnp.logical_not(at_start & (p == 0)))(copy.wait_send)

    each(0, groups, return_left)
    each(0, groups, return_own)
    solved_rx[g] = solved_tx[g // per_block]
    loaded(14, 15)
    own_choices = choices(owner_ref[...], g)
    right_choices = choices(owner_right, g_right)

    def back_own(d):
        p = lax.rem(g + d, groups)
        remote(solved_tx.at[0], solved_rx.at[p], solved_send.at[p], solved_recv.at[p], (p, m)).wait()

    def back_next(p):
        remote(
            solved_tx.at[0], solved_rx.at[groups + p], solved_send.at[groups + p], solved_recv.at[groups + p], right
        ).wait_recv()

    each(1, groups, back_own)

    @pl.when(jnp.logical_not(is_last))
    def _():
        each(0, groups, back_next)


    def corrections(start, chosen, mask):
        at_row = iota((owner_rows, wide), 0)
        gathered = jnp.zeros((owner_rows, wide), F32)
        for p in range(groups):
            gathered = jnp.where(at_row == p, jnp.broadcast_to(solved_rx[start + p], gathered.shape), gathered)
        values = stacked_exact(gathered, chosen, dot)
        values = [values[:, c * vertices : (c + 1) * vertices] for c in range(3)]
        return [jnp.sum(jnp.where(mask, t, 0.0), axis=0, keepdims=True) for t in values]

    own_correction = corrections(0, *own_choices)
    next_correction = [jnp.where(is_last, 0.0, t) for t in corrections(groups, *right_choices)]
    rows = []
    for c in range(3):
        rows.append(jnp.broadcast_to(own_correction[c], (8, vertices)))
        rows.append(jnp.broadcast_to(next_correction[c], (8, vertices)))
    rows = jnp.where(vertex_mask, jnp.concatenate(rows, axis=0), 0.0)
    rows = times_right(rows, hatzp_ref[...])
    rows = jnp.concatenate([rows[16 * c : 16 * c + 16] for c in range(3)], axis=1)
    update = times_left(hatst_ref[...], rows)
    new_direction, beyond_new = [], []
    for c in range(3):
        part = update[:, c * lanes : (c + 1) * lanes]
        new_direction.append(own_direction[c] + keep * part[: 4 * ny])
        beyond_new.append(beyond_direction[c] + keep_right * part[4 * ny :])
        new_ref[c] = new_direction[c].reshape(4, ny, lanes)
    store_new = pltpu.make_async_copy(new_ref, outputs[0], store_sem.at[0])
    store_new.start()
    beyond_new = [jnp.where(is_last, 0.0, t) for t in beyond_new]
    whole_z = along_z([t for c in range(3) for t in (keep * new_direction[c], beyond_new[c])])
    gradients([whole_z[c * 5 * ny : (c + 1) * 5 * ny] for c in range(3)], ((gvb, gvz),))
    fluxes(False)
    image = divergence()
    for c in range(3):
        last_tx[c * ny : (c + 1) * ny, :] = image[4 * ny :, c * lanes : (c + 1) * lanes]
    copy_layer = remote(
        last_tx.at[pl.ds(0, 3 * ny)], last_rx.at[pl.ds(0, 3 * ny)], last_send.at[0], last_recv.at[0], right
    )
    pl.when(jnp.logical_not(is_last))(copy_layer.start)
    own_last, beyond_last = settle(image, new_direction)
    low_sums, high_sums = restrict(widened(own_last, beyond_last))
    last_tx[3 * ny :, :] = high_sums
    copy_sums = remote(
        last_tx.at[pl.ds(3 * ny, 8)], last_rx.at[pl.ds(3 * ny, 8)], last_send.at[1], last_recv.at[1], right
    )
    pl.when(jnp.logical_not(is_last))(copy_sums.start)
    for c in range(3):
        residual_ref[c, 1:] = own_last[c][ny:].reshape(3, ny, lanes)
    store_rest = pltpu.make_async_copy(residual_ref.at[:, 1:], outputs[1].at[:, 1:], store_sem.at[1])
    store_rest.start()
    pl.when(jnp.logical_not(is_first))(copy_layer.wait_recv)
    for c in range(3):
        arrived = jnp.where(is_first, 0.0, last_rx[c * ny : (c + 1) * ny, :])
        residual_ref[c, 0] = own_last[c][:ny] - keep[:ny] * arrived
    store_first = pltpu.make_async_copy(residual_ref.at[:, 0], outputs[1].at[:, 0], store_sem.at[2])
    store_first.start()
    pl.when(jnp.logical_not(is_first))(copy_sums.wait_recv)
    total = low_sums + jnp.where(is_first, 0.0, last_rx[3 * ny :, :])
    for c in range(3):
        for k in range(count_y):
            coarse_ref[c, 0, k : k + 1, :] = total[c : c + 1, k * count_z : (k + 1) * count_z]
    store_coarse = pltpu.make_async_copy(coarse_ref, outputs[2], store_sem.at[3])
    store_coarse.start()
    each(0, groups, left_sent)

    @pl.when(jnp.logical_not(is_first))
    def _():
        for copy in halo:
            copy.wait_send()

    @pl.when(jnp.logical_not(is_last))
    def _():
        each(0, groups, lambda p: next_copy(p).wait_send())
        copy_layer.wait_send()
        copy_sums.wait_send()

    for copy in (store_new, store_rest, store_first, store_coarse):
        copy.wait()


def write_out(*refs):
    sources, targets, held, sems = refs[:3], refs[3:6], refs[6:9], refs[9]
    loads = [pltpu.make_async_copy(a, b, sems.at[i]) for i, (a, b) in enumerate(zip(sources, held))]
    stores = [pltpu.make_async_copy(a, b, sems.at[3 + i]) for i, (a, b) in enumerate(zip(held, targets))]
    for copy in loads:
        copy.start()
    for load, store in zip(loads, stores):
        load.wait()
        store.start()
    for copy in stores:
        copy.wait()


def shards(groups, members, state, direction, rhs, clamp, stiffness, coarse_owner, coarse_inverse):
    count_y, count_z = stiffness.shape[1:]
    ny, nz = 4 * count_y, 4 * count_z
    tables = [jnp.asarray(t.astype(np.float32)) for t in constant_tables(count_y, count_z)]
    blocks, size = coarse_inverse.shape[1:3]
    wide = -(-size // 128) * 128
    vertices = count_y * count_z
    results = tuple(
        jax.ShapeDtypeStruct(t, F32) for t in (state.shape, state.shape, (3, 1, count_y, count_z))
    )
    operands = [state, direction, rhs, clamp, stiffness, coarse_owner, coarse_inverse, *tables]
    new, residual, coarse = pl.pallas_call(
        functools.partial(kernel, groups, members),
        out_shape=results,
        in_specs=[pl.BlockSpec(memory_space=pl.ANY)] * INPUTS,
        out_specs=[pl.BlockSpec(memory_space=pl.ANY)] * 3,
        scratch_shapes=[pltpu.VMEM(t.shape, t.dtype) for t in operands]
        + [pltpu.VMEM(t.shape, F32) for t in results]
        + [
            pltpu.VMEM((t.shape[0] * by_rows, t.shape[1] * by_columns), BF16)
            for t, by_rows, by_columns in zip(tables, (1, 3, 1, 1, 1, 1, 3, 3, 1), (1, 1, 2, 2, 1, 1, 1, 1, 1))
        ]
        + [
            pltpu.VMEM(clamp.shape, jnp.int32),
            pltpu.VMEM(coarse_owner.shape, jnp.int32),
            pltpu.VMEM((3, ny, nz), F32),
            pltpu.VMEM((3, ny, nz), F32),
            pltpu.VMEM((2, 8, vertices), F32),
            pltpu.VMEM((2 * groups, 8, vertices), F32),
            pltpu.VMEM((blocks, 1, wide), F32),
            pltpu.VMEM((2 * groups, 1, wide), F32),
            pltpu.VMEM((3 * ny + 8, nz), F32),
            pltpu.VMEM((3 * ny + 8, nz), F32),
            pltpu.VMEM((blocks, wide, wide), BF16),
            pltpu.VMEM((blocks, wide, wide), BF16),
            pltpu.VMEM((NQ, 256), F32),
            pltpu.VMEM((2 * NQ, 768), F32),
            pltpu.VMEM((NQ, 768), F32),
            pltpu.VMEM((2 * NQ, 768), F32),
            pltpu.VMEM((NQ, 768), F32),
            pltpu.VMEM((9, NQ, 256), F32),
            pltpu.VMEM((6, NQ, 256), F32),
            pltpu.VMEM((6 * NQ, 256), BF16),
            pltpu.VMEM((6 * NQ, 256), BF16),
            pltpu.VMEM((3 * NQ, 256), BF16),
            pltpu.VMEM((3 * NQ, 256), BF16),
            pltpu.SemaphoreType.DMA((4,)),
            pltpu.SemaphoreType.DMA((4,)),
            pltpu.SemaphoreType.DMA((2 * groups,)),
            pltpu.SemaphoreType.DMA((2 * groups,)),
            pltpu.SemaphoreType.DMA((2 * groups,)),
            pltpu.SemaphoreType.DMA((2 * groups,)),
            pltpu.SemaphoreType.DMA((2,)),
            pltpu.SemaphoreType.DMA((2,)),
            pltpu.SemaphoreType.DMA((INPUTS,)),
            pltpu.SemaphoreType.DMA((4,)),
        ],
        compiler_params=pltpu.CompilerParams(
            collective_id=0, has_side_effects=True, vmem_limit_bytes=56 * 1024 * 1024
        ),
    )(*operands)
    return pl.pallas_call(
        write_out,
        out_shape=results,
        in_specs=[pl.BlockSpec(memory_space=pl.ANY)] * 3,
        out_specs=[pl.BlockSpec(memory_space=pl.ANY)] * 3,
        scratch_shapes=[pltpu.VMEM(t.shape, F32) for t in results] + [pltpu.SemaphoreType.DMA((6,))],
        compiler_params=pltpu.CompilerParams(vmem_limit_bytes=56 * 1024 * 1024),
    )(new, residual, coarse)


def solution(mesh):
    in_specs = (
        P(None, ("grp", "mem"), None, None),
        P(None, ("grp", "mem"), None, None),
        P(None, ("grp", "mem"), None, None),
        P(("grp", "mem"), None),
        P(("grp", "mem"), None, None),
        P(("grp", "mem"), None),
        P(("grp", "mem"), None, None, None),
    )
    out_specs = (
        P(None, ("grp", "mem"), None, None),
        P(None, ("grp", "mem"), None, None),
        P(None, ("grp", "mem"), None, None),
    )
    body = functools.partial(shards, mesh.shape["grp"], mesh.shape["mem"])
    return jax.shard_map(body, mesh=mesh, in_specs=in_specs, out_specs=out_specs, check_vma=False)
```

```python
import functools

import jax
import jax.numpy as jnp
import ml_dtypes
import numpy as np
from jax import lax
from jax.experimental import pallas as pl
from jax.experimental.pallas import tpu as pltpu
from jax.sharding import PartitionSpec as P

LAME_FIRST = 1.2
LAME_SHEAR = 0.8
HIGHEST = lax.Precision.HIGHEST
MESH = pl.DeviceIdType.MESH
F32 = jnp.float32
BF16 = jnp.bfloat16
INPUTS = 18
NQ = 112


def gauss_rule():
    inner = np.sqrt(5.0 - 2.0 * np.sqrt(10.0 / 7.0)) / 3.0
    outer = np.sqrt(5.0 + 2.0 * np.sqrt(10.0 / 7.0)) / 3.0
    inner_weight = (322.0 + 13.0 * np.sqrt(70.0)) / 900.0
    outer_weight = (322.0 - 13.0 * np.sqrt(70.0)) / 900.0
    points = np.array([-outer, -inner, 0.0, inner, outer])
    weights = np.array([outer_weight, inner_weight, 128.0 / 225.0, inner_weight, outer_weight])
    return (points, weights)


def basis_tables():
    gll_points = np.array([-1.0, -np.sqrt(3.0 / 7.0), 0.0, np.sqrt(3.0 / 7.0), 1.0])
    gauss_points, gauss_weights = gauss_rule()
    values = np.zeros((5, 5))
    slopes = np.zeros((5, 5))
    for j in range(5):
        others = [gll_points[k] for k in range(5) if k != j]
        denominator = np.prod([gll_points[j] - o for o in others])
        for q in range(5):
            t = gauss_points[q]
            values[q, j] = np.prod([t - o for o in others]) / denominator
            total = 0.0
            for i in range(4):
                total += np.prod([t - others[k] for k in range(4) if k != i])
            slopes[q, j] = 2.0 * total / denominator
    return (gll_points, gauss_weights, values, slopes)


def banded(table, count):
    banded_matrix = np.zeros((5 * count, 4 * count + 1))
    for e in range(count):
        banded_matrix[5 * e : 5 * e + 5, 4 * e : 4 * e + 5] = table
    return banded_matrix[:, :-1]


def restrictor(gll_points, count):
    result = np.zeros((count, 4 * count))
    for e in range(count):
        for j in range(4):
            result[e, 4 * e + j] += (1.0 - gll_points[j]) / 2.0
            if e + 1 < count:
                result[e + 1, 4 * e + j] += (1.0 + gll_points[j]) / 2.0
    return result


def halves(table):
    high = table.astype(ml_dtypes.bfloat16)
    low = (table - high.astype(np.float64)).astype(ml_dtypes.bfloat16)
    return high, low


def padded(table, axis, multiple):
    widths = [(0, 0), (0, 0)]
    widths[axis] = (0, -table.shape[axis] % multiple)
    return np.pad(table, widths)


def left_table(table):
    high, low = halves(table)
    return padded(np.concatenate([high, high, low], axis=1), 1, 128)


def constant_tables(count_y, count_z):
    gll_points, weights, values, slopes = basis_tables()
    by, dy = banded(values, count_y), banded(slopes, count_y)
    bz, dz = banded(values, count_z), banded(slopes, count_z)
    pads = lambda t: np.pad(t, ((0, NQ - t.shape[0]), (0, 0)))
    cross = np.concatenate(
        [pads(np.kron(slopes, by)), pads(np.kron(values, dy)), pads(np.kron(values, by))]
    )
    bz, dz = padded(bz, 0, 256), padded(dz, 0, 256)
    low_hat = np.append((1.0 - gll_points[:4]) / 2.0, 0.0)
    high_hat = np.append((1.0 + gll_points[:4]) / 2.0, 1.0)
    hat_y = restrictor(gll_points, count_y)
    hat_z = restrictor(gll_points, count_z)
    hats = np.zeros((16, 20 * count_y))
    hats[:count_y] = np.kron(low_hat[None], hat_y)
    hats[8 : 8 + count_y] = np.kron(high_hat[None], hat_y)
    tiled = np.tile(hat_z, (count_y, 1))
    spread_y = np.zeros((NQ, count_y))
    spread_y[:100] = np.kron(weights[:, None], np.kron(np.eye(count_y), weights[:, None])) / 8.0
    spread_z = padded(np.kron(np.eye(count_z), weights[None]), 1, 256)
    return (
        left_table(cross),
        np.concatenate([bz.T, dz.T], axis=1),
        bz,
        dz,
        left_table(cross.T),
        left_table(hats),
        tiled.T,
        tiled,
        left_table(hats.T),
        spread_y.astype(np.float32),
        spread_z.astype(np.float32),
    )


def split(x):
    high = x.astype(BF16)
    return high, (x - high.astype(F32)).astype(BF16)


def dot(a, b):
    return lax.dot_general(a, b, (((1,), (0,)), ((), ())), preferred_element_type=F32)


def dot_nt(a, b):
    return lax.dot_general(a, b, (((1,), (1,)), ((), ())), preferred_element_type=F32)


def times_right(x, table):
    high, low = split(x)
    return dot(jnp.concatenate([high, low, high], axis=1), table)


def times_left(table, x):
    high, low = split(x)
    parts = [high, low, high]
    rest = table.shape[1] - 3 * x.shape[0]
    if rest:
        parts.append(jnp.zeros((rest, x.shape[1]), BF16))
    return dot(table, jnp.concatenate(parts, axis=0))


def stacked_exact(x, one_hot, product):
    rows = x.shape[0]
    high, low = split(x)
    both = product(jnp.concatenate([high, low], axis=0), one_hot)
    return both[:rows] + both[rows:]


def iota(shape, axis):
    return lax.broadcasted_iota(jnp.int32, shape, axis)


def each(low, high, act):
    if high - low <= 8:
        for i in range(low, high):
            act(i)
    else:

        def step(i, carry):
            act(i)
            return carry

        lax.fori_loop(low, high, step, 0)


def kernel(groups, members, *refs):
    sources, outputs = refs[:INPUTS], refs[INPUTS : INPUTS + 3]
    local, scratch = refs[INPUTS + 3 : 2 * INPUTS + 3], refs[2 * INPUTS + 3 :]
    state_ref, direction_ref, rhs_ref, clamp_ref, stiff_ref, owner_ref, inverse_ref = local[:7]
    spready_ref, spreadz_ref = local[16:]
    new_ref, residual_ref, coarse_ref = scratch[:3]
    narrow = scratch[3:12]
    cross_ref, bdz_ref, bzt_ref, dzt_ref, crosst_ref, hats_ref, hatz_ref, hatzp_ref, hatst_ref = narrow
    (
        halo_clamp,
        halo_owner,
        halo_state,
        halo_rx,
        sums_tx,
        sums_rx,
        solved_tx,
        solved_rx,
        last_tx,
        last_rx,
        inv_high,
        inv_low,
        weight,
        gsb,
        gsz,
        gvb,
        gvz,
        deform_s,
        stress_s,
        fbh,
        fbl,
        fzh,
        fzl,
        halo_send,
        halo_recv,
        sums_send,
        sums_recv,
        solved_send,
        solved_recv,
        last_send,
        last_recv,
        load_sem,
        store_sem,
    ) = scratch[12:]
    count_y, count_z = stiff_ref.shape[1:]
    ny = 4 * count_y
    vertices = count_y * count_z
    blocks = inverse_ref.shape[1]
    size = inverse_ref.shape[2]
    block = size // 3
    message = vertices // groups
    per_block = groups // blocks
    g = lax.axis_index("grp")
    m = lax.axis_index("mem")
    m_right = lax.rem(m + 1, members)
    m_left = lax.rem(m + members - 1, members)
    at_end = m == members - 1
    at_start = m == 0
    g_right = lax.rem(g + at_end.astype(jnp.int32), groups)
    g_left = lax.rem(g + groups - at_start.astype(jnp.int32), groups)
    is_last = (g * members + m) == groups * members - 1
    is_first = (g * members + m) == 0

    barrier = pltpu.get_barrier_semaphore()

    def greet(p, member):
        pl.semaphore_signal(barrier, inc=1, device_id=(p, member), device_id_type=MESH)

    greet(g_left, m_left)
    each(1, groups, lambda d: greet(lax.rem(g_left + d, groups), m_left))
    each(0, groups, lambda d: greet(lax.rem(g_right + d, groups), m_right))
    each(1, groups, lambda d: greet(lax.rem(g + d, groups), m))
    loads = [pltpu.make_async_copy(a, b, load_sem.at[i]) for i, (a, b) in enumerate(zip(sources, local))]
    order = [3, 5, 1, 0, 8, 4, 16, 17, 7, 9, 10, 11, 2, 12, 13, 6]
    for i in order + [i for i in range(INPUTS) if i not in order]:
        loads[i].start()

    def loaded(*which):
        for i in which:
            loads[i].wait()
            if 7 <= i < 16:
                target = narrow[i - 7]
                rows, columns = local[i].shape
                if target.shape == local[i].shape:
                    target[...] = local[i][...].astype(BF16)
                    continue
                high, low = split(local[i][...])
                target[:rows, :columns] = high
                if target.shape[0] == rows:
                    target[:, columns:] = low
                else:
                    target[rows : 2 * rows, :] = high
                    target[2 * rows :, :] = low

    pl.semaphore_wait(barrier, 3 * groups - 1)

    def along_z(parts):
        return times_right(jnp.concatenate(parts, axis=0), bdz_ref[...])

    left = (g_left, m_left)
    right = (g_right, m_right)

    def remote(src, dst, send, recv, device):
        return pltpu.make_async_remote_copy(
            src_ref=src, dst_ref=dst, send_sem=send, recv_sem=recv, device_id=device, device_id_type=MESH
        )

    halo = [
        remote(a, b, halo_send.at[i], halo_recv.at[i], left)
        for i, (a, b) in enumerate(
            (
                (sources[0].at[:, 0], halo_state),
                (sources[1].at[:, 0], halo_rx),
                (sources[3], halo_clamp),
                (sources[5], halo_owner),
            )
        )
    ]

    @pl.when(jnp.logical_not(is_first))
    def _():
        for copy in halo:
            copy.start()

    def clamp_column(ref, x):
        row = jnp.broadcast_to(ref[x : x + 1, :].astype(F32), (ny, ny))
        return jnp.sum(jnp.where(iota((ny, ny), 0) == iota((ny, ny), 1), row, 0.0), axis=1, keepdims=True)

    def keep_of(column):
        shape = (column.shape[0], lanes)
        return jnp.where(iota(shape, 1) == 0, jnp.broadcast_to(1.0 - column, shape), 1.0)

    lanes = 4 * count_z
    loaded(3, 5, 1)
    keep = keep_of(jnp.concatenate([clamp_column(clamp_ref, x) for x in range(4)], axis=0))

    loaded(0, 8)
    own_state = [state_ref[c].reshape(4 * ny, lanes) for c in range(3)]
    own_direction = [direction_ref[c].reshape(4 * ny, lanes) for c in range(3)]
    own_z = along_z(own_state + [keep * t for t in own_direction])
    sums_rx[:, 4:, :] = jnp.zeros((2 * groups, 4, vertices), F32)
    loaded(4, 16, 17, 7)
    along_y = jnp.zeros((NQ, count_z), F32)
    for k in range(count_y):
        along_y = along_y + spready_ref[:, k : k + 1] * stiff_ref[0, k : k + 1, :]
    weight[...] = jnp.dot(along_y, spreadz_ref[...], precision=HIGHEST, preferred_element_type=F32)
    own_hot = (owner_ref[...] == iota((vertices, vertices), 0)).astype(F32).astype(BF16)

    wide = inv_high.shape[2]
    owner_rows = -(-groups // 8) * 8

    def choices(owner, group):
        place = lax.rem(group, per_block) * message + lax.rem(owner, message)
        rows = iota((wide, vertices), 0)
        chosen = jnp.concatenate([rows == c * block + place for c in range(3)], axis=1)
        return chosen.astype(F32).astype(BF16), iota((owner_rows, vertices), 0) == owner // message

    def gradients(columns, targets):
        for first, rows, place in ((0, pl.ds(0, 2 * NQ), 0), (256, pl.ds(2 * NQ, NQ), 1)):
            wide_field = jnp.concatenate([t[:, first : first + 256] for t in columns], axis=1)
            result = times_left(cross_ref[rows, :], wide_field)
            for i, target in enumerate(targets):
                target[place][...] = result[:, i * 768 : (i + 1) * 768]

    def load_change(from_b, from_z, r, half):
        change = []
        for c in range(3):
            s = pl.ds(c * 256 + half * 128, 128)
            change.append(
                [
                    from_b[pl.ds(r, 16), s],
                    from_b[pl.ds(pl.multiple_of(NQ + r, 16), 16), s],
                    from_z[pl.ds(r, 16), s],
                ]
            )
        return change

    pairs = [(0, 0), (1, 1), (2, 2), (0, 1), (0, 2), (1, 2)]

    def fluxes(first):
        def body(i, carry):
            r = pl.multiple_of(i * 16, 16)
            for half in range(2):
                s = pl.ds(half * 128, 128)
                w = weight[pl.ds(r, 16), s]
                if first:
                    grad = load_change(gsb, gsz, r, half)
                    deform = [[grad[c][a] + 1.0 if c == a else grad[c][a] for a in range(3)] for c in range(3)]
                    cg = [sum(deform[k][a] * deform[k][b] for k in range(3)) for a, b in pairs]
                    trace = (0.5 * LAME_FIRST) * (cg[0] + cg[1] + cg[2]) - 1.5 * LAME_FIRST
                    stress = [LAME_SHEAR * t for t in cg]
                    stress = [w * (t - LAME_SHEAR + trace) for t in stress[:3]] + [w * t for t in stress[3:]]
                    for c in range(3):
                        for a in range(3):
                            deform_s[3 * c + a, pl.ds(r, 16), s] = deform[c][a]
                    for k in range(6):
                        stress_s[k, pl.ds(r, 16), s] = stress[k]
                else:
                    deform = [[deform_s[3 * c + a, pl.ds(r, 16), s] for a in range(3)] for c in range(3)]
                    stress = [stress_s[k, pl.ds(r, 16), s] for k in range(6)]
                change = load_change(gvb, gvz, r, half)
                diagonal = [sum(deform[k][a] * change[k][a] for k in range(3)) for a in range(3)]
                trace = LAME_FIRST * (diagonal[0] + diagonal[1] + diagonal[2])
                moved = [w * (2.0 * LAME_SHEAR * t + trace) for t in diagonal]
                shear = LAME_SHEAR * w
                for a, b in pairs[3:]:
                    moved.append(
                        shear * sum(deform[k][a] * change[k][b] + deform[k][b] * change[k][a] for k in range(3))
                    )
                at = [[0, 3, 4], [3, 1, 5], [4, 5, 2]]
                for c in range(3):
                    for a in range(3):
                        entry = sum(change[c][b] * stress[at[b][a]] + deform[c][b] * moved[at[b][a]] for b in range(3))
                        high, low = split(entry)
                        if a < 2:
                            place = pl.ds(pl.multiple_of(c * 2 * NQ + a * NQ + r, 16), 16)
                            fbh[place, s] = high
                            fbl[place, s] = low
                        else:
                            place = pl.ds(pl.multiple_of(c * NQ + r, 16), 16)
                            fzh[place, s] = high
                            fzl[place, s] = low
            return carry

        lax.fori_loop(0, NQ // 16, body, 0, unroll=True)

    def divergence():
        both_b = dot(fbh[...], bzt_ref[...])
        both_z = dot(fzh[...], dzt_ref[...])
        side_b = both_b[:, :lanes] + both_b[:, lanes:] + dot(fbl[...], bzt_ref[:, :lanes])
        side_z = both_z[:, :lanes] + both_z[:, lanes:] + dot(fzl[...], dzt_ref[:, :lanes])
        columns = [
            jnp.concatenate([side_b[c * 2 * NQ : (c + 1) * 2 * NQ], side_z[c * NQ : (c + 1) * NQ]], axis=0)
            for c in range(3)
        ]
        return times_left(crosst_ref[...], jnp.concatenate(columns, axis=1))

    vertex_of_row = lax.rem(iota((48, vertices), 0), 8)
    vertex_mask = vertex_of_row == iota((48, vertices), 1) // count_z

    def restrict(field):
        rows = times_left(hats_ref[...], field)
        rows = jnp.concatenate([rows[:, c * lanes : (c + 1) * lanes] for c in range(3)], axis=0)
        rows = jnp.where(vertex_mask, times_right(rows, hatz_ref[...]), 0.0)
        rows = [jnp.sum(rows[8 * i : 8 * i + 8], axis=0, keepdims=True) for i in range(6)]
        fill = jnp.zeros((5, vertices), F32)
        return (
            jnp.concatenate([rows[0], rows[2], rows[4], fill], axis=0),
            jnp.concatenate([rows[1], rows[3], rows[5], fill], axis=0),
        )

    def widened(own, beyond):
        return jnp.concatenate([jnp.concatenate([own[c], beyond[c]], axis=0) for c in range(3)], axis=1)

    loaded(2, 9, 10, 11, 12, 13)
    own_rhs = [rhs_ref[c].reshape(4 * ny, lanes) for c in range(3)]

    @pl.when(jnp.logical_not(is_last))
    def _():
        for copy in halo:
            copy.wait_recv()

    beyond_state = [jnp.where(is_last, 0.0, halo_state[c]) for c in range(3)]
    keep_right = jnp.where(is_last, 0.0, keep_of(clamp_column(halo_clamp, 0)))
    beyond_direction = [jnp.where(is_last, 0.0, keep_right * halo_rx[c]) for c in range(3)]
    owner_right = halo_owner[...]
    right_hot = (owner_right == iota((vertices, vertices), 0)).astype(F32).astype(BF16)
    beyond_z = along_z(beyond_state + beyond_direction)
    columns = [
        jnp.concatenate([own_z[i * 4 * ny : (i + 1) * 4 * ny], beyond_z[i * ny : (i + 1) * ny]], axis=0)
        for i in range(6)
    ]
    gradients(columns, ((gsb, gsz), (gvb, gvz)))
    fluxes(True)
    image = divergence()

    def settle(image, field):
        own, beyond = [], []
        for c in range(3):
            part = image[:, c * lanes : (c + 1) * lanes]
            own.append(own_rhs[c] - keep * part[: 4 * ny] - (1.0 - keep) * field[c])
            beyond.append(-keep_right * part[4 * ny :])
        return own, beyond

    own_first, beyond_first = settle(image, own_direction)
    low_sums, high_sums = restrict(widened(own_first, beyond_first))
    high_sums = jnp.where(is_last, 0.0, high_sums)
    sums_tx[0] = stacked_exact(low_sums, own_hot, dot_nt)
    sums_tx[1] = stacked_exact(high_sums, right_hot, dot_nt)

    def far(i):
        return jnp.where(g >= groups // 2, i, groups - 1 - i)

    def send_own(i):
        p = far(i)

        @pl.when(p != g)
        def _():
            remote(
                sums_tx.at[0, pl.ds(0, 4)], sums_rx.at[g, pl.ds(0, 4)], sums_send.at[p], sums_recv.at[g], (p, m)
            ).start()

    def send_next(i):
        p = far(i)
        remote(
            sums_tx.at[1, pl.ds(0, 4)],
            sums_rx.at[groups + g_right, pl.ds(0, 4)],
            sums_send.at[groups + p],
            sums_recv.at[groups + g_right],
            (p, m_right),
        ).start()

    @pl.when(jnp.logical_not(is_last))
    def _():
        each(0, groups, send_next)

    each(0, groups, send_own)
    sums_rx[g] = sums_tx[0]

    @pl.when(at_start)
    def _():
        sums_rx[groups] = jnp.zeros((8, vertices), F32)

    loaded(6)
    inv_high[...] = jnp.zeros_like(inv_high)
    inv_low[...] = jnp.zeros_like(inv_low)
    for b in range(blocks):
        high, low = split(inverse_ref[0, b])
        inv_high[b, :size, :size] = high
        inv_low[b, :size, :size] = low
    pick = (
        iota((vertices, wide), 0) == g * message + lax.rem(iota((vertices, wide), 1), message)
    ).astype(F32).astype(BF16)
    shape = (groups * 8, wide)
    row, lane = iota(shape, 0), iota(shape, 1)
    pick_mask = (
        (lane // block == lax.rem(row, 8))
        & (lax.rem(lane, block) // message == lax.rem(row // 8, per_block))
        & (lane < size)
    )

    def got_own(d):
        p = lax.rem(g + d, groups)
        remote(
            sums_tx.at[0, pl.ds(0, 4)], sums_rx.at[p, pl.ds(0, 4)], sums_send.at[p], sums_recv.at[p], (p, m)
        ).wait()

    def next_copy(p):
        return remote(
            sums_tx.at[1, pl.ds(0, 4)],
            sums_rx.at[groups + p, pl.ds(0, 4)],
            sums_send.at[groups + p],
            sums_recv.at[groups + p],
            right,
        )

    def got_next(p):
        @pl.when(jnp.logical_not(at_start & (p == 0)))
        def _():
            next_copy(p).wait_recv()

    each(1, groups, got_own)
    each(0, groups, got_next)

    received = sums_rx[:groups] + sums_rx[groups:]
    received = received.reshape(groups * 8, vertices)
    placed = jnp.where(pick_mask, stacked_exact(received, pick, dot), 0.0)
    vectors = [
        jnp.sum(placed[b * per_block * 8 : (b + 1) * per_block * 8], axis=0, keepdims=True) for b in range(blocks)
    ]
    for b in range(blocks):
        high, low = split(jnp.broadcast_to(vectors[b], (8, wide)))
        both = dot_nt(jnp.concatenate([high, low], axis=0), inv_high[b])
        solved_tx[b] = (both[:1] + both[8:9]) + dot_nt(jnp.concatenate([high, high], axis=0), inv_low[b])[:1]

    def return_own(i):
        p = far(i)

        @pl.when(p != g)
        def _():
            remote(
                solved_tx.at[p // per_block], solved_rx.at[g], solved_send.at[p], solved_recv.at[g], (p, m)
            ).start()

    def left_copy(i):
        p = far(i)
        before = lax.rem(p + groups - at_start.astype(jnp.int32), groups)
        return p, remote(
            solved_tx.at[p // per_block],
            solved_rx.at[groups + g],
            solved_send.at[groups + p],
            solved_recv.at[groups + g],
            (before, m_left),
        )

    def return_left(d):
        p, copy = left_copy(d)
        pl.when(jnp.logical_not(at_start & (p == 0)))(copy.start)

    def left_sent(d):
        p, copy = left_copy(d)
        pl.when(jnp.logical_not(at_start & (p == 0)))(copy.wait_send)

    each(0, groups, return_left)
    each(0, groups, return_own)
    solved_rx[g] = solved_tx[g // per_block]
    loaded(14, 15)
    own_choices = choices(owner_ref[...], g)
    right_choices = choices(owner_right, g_right)

    def back_own(d):
        p = lax.rem(g + d, groups)
        remote(solved_tx.at[0], solved_rx.at[p], solved_send.at[p], solved_recv.at[p], (p, m)).wait()

    def back_next(p):
        remote(
            solved_tx.at[0], solved_rx.at[groups + p], solved_send.at[groups + p], solved_recv.at[groups + p], right
        ).wait_recv()

    each(1, groups, back_own)

    @pl.when(jnp.logical_not(is_last))
    def _():
        each(0, groups, back_next)


    def corrections(start, chosen, mask):
        at_row = iota((owner_rows, wide), 0)
        gathered = jnp.zeros((owner_rows, wide), F32)
        for p in range(groups):
            gathered = jnp.where(at_row == p, jnp.broadcast_to(solved_rx[start + p], gathered.shape), gathered)
        values = stacked_exact(gathered, chosen, dot)
        values = [values[:, c * vertices : (c + 1) * vertices] for c in range(3)]
        return [jnp.sum(jnp.where(mask, t, 0.0), axis=0, keepdims=True) for t in values]

    own_correction = corrections(0, *own_choices)
    next_correction = [jnp.where(is_last, 0.0, t) for t in corrections(groups, *right_choices)]
    rows = []
    for c in range(3):
        rows.append(jnp.broadcast_to(own_correction[c], (8, vertices)))
        rows.append(jnp.broadcast_to(next_correction[c], (8, vertices)))
    rows = jnp.where(vertex_mask, jnp.concatenate(rows, axis=0), 0.0)
    rows = times_right(rows, hatzp_ref[...])
    rows = jnp.concatenate([rows[16 * c : 16 * c + 16] for c in range(3)], axis=1)
    update = times_left(hatst_ref[...], rows)
    new_direction, beyond_new = [], []
    for c in range(3):
        part = update[:, c * lanes : (c + 1) * lanes]
        new_direction.append(own_direction[c] + keep * part[: 4 * ny])
        beyond_new.append(beyond_direction[c] + keep_right * part[4 * ny :])
        new_ref[c] = new_direction[c].reshape(4, ny, lanes)
    store_new = pltpu.make_async_copy(new_ref, outputs[0], store_sem.at[0])
    store_new.start()
    beyond_new = [jnp.where(is_last, 0.0, t) for t in beyond_new]
    whole_z = along_z([t for c in range(3) for t in (keep * new_direction[c], beyond_new[c])])
    gradients([whole_z[c * 5 * ny : (c + 1) * 5 * ny] for c in range(3)], ((gvb, gvz),))
    fluxes(False)
    image = divergence()
    for c in range(3):
        last_tx[c * ny : (c + 1) * ny, :] = image[4 * ny :, c * lanes : (c + 1) * lanes]
    copy_layer = remote(
        last_tx.at[pl.ds(0, 3 * ny)], last_rx.at[pl.ds(0, 3 * ny)], last_send.at[0], last_recv.at[0], right
    )
    pl.when(jnp.logical_not(is_last))(copy_layer.start)
    own_last, beyond_last = settle(image, new_direction)
    low_sums, high_sums = restrict(widened(own_last, beyond_last))
    last_tx[3 * ny :, :] = high_sums
    copy_sums = remote(
        last_tx.at[pl.ds(3 * ny, 8)], last_rx.at[pl.ds(3 * ny, 8)], last_send.at[1], last_recv.at[1], right
    )
    pl.when(jnp.logical_not(is_last))(copy_sums.start)
    for c in range(3):
        residual_ref[c, 1:] = own_last[c][ny:].reshape(3, ny, lanes)
    store_rest = pltpu.make_async_copy(residual_ref.at[:, 1:], outputs[1].at[:, 1:], store_sem.at[1])
    store_rest.start()
    pl.when(jnp.logical_not(is_first))(copy_layer.wait_recv)
    for c in range(3):
        arrived = jnp.where(is_first, 0.0, last_rx[c * ny : (c + 1) * ny, :])
        residual_ref[c, 0] = own_last[c][:ny] - keep[:ny] * arrived
    store_first = pltpu.make_async_copy(residual_ref.at[:, 0], outputs[1].at[:, 0], store_sem.at[2])
    store_first.start()
    pl.when(jnp.logical_not(is_first))(copy_sums.wait_recv)
    total = low_sums + jnp.where(is_first, 0.0, last_rx[3 * ny :, :])
    for c in range(3):
        for k in range(count_y):
            coarse_ref[c, 0, k : k + 1, :] = total[c : c + 1, k * count_z : (k + 1) * count_z]
    store_coarse = pltpu.make_async_copy(coarse_ref, outputs[2], store_sem.at[3])
    store_coarse.start()
    each(0, groups, left_sent)

    @pl.when(jnp.logical_not(is_first))
    def _():
        for copy in halo:
            copy.wait_send()

    @pl.when(jnp.logical_not(is_last))
    def _():
        each(0, groups, lambda p: next_copy(p).wait_send())
        copy_layer.wait_send()
        copy_sums.wait_send()

    for copy in (store_new, store_rest, store_first, store_coarse):
        copy.wait()


def write_out(*refs):
    sources, targets, held, sems = refs[:3], refs[3:6], refs[6:9], refs[9]
    loads = [pltpu.make_async_copy(a, b, sems.at[i]) for i, (a, b) in enumerate(zip(sources, held))]
    stores = [pltpu.make_async_copy(a, b, sems.at[3 + i]) for i, (a, b) in enumerate(zip(held, targets))]
    for copy in loads:
        copy.start()
    for load, store in zip(loads, stores):
        load.wait()
        store.start()
    for copy in stores:
        copy.wait()


def shards(groups, members, state, direction, rhs, clamp, stiffness, coarse_owner, coarse_inverse):
    count_y, count_z = stiffness.shape[1:]
    ny, nz = 4 * count_y, 4 * count_z
    tables = [jnp.asarray(t.astype(np.float32)) for t in constant_tables(count_y, count_z)]
    blocks, size = coarse_inverse.shape[1:3]
    wide = -(-size // 128) * 128
    vertices = count_y * count_z
    results = tuple(
        jax.ShapeDtypeStruct(t, F32) for t in (state.shape, state.shape, (3, 1, count_y, count_z))
    )
    operands = [state, direction, rhs, clamp, stiffness, coarse_owner, coarse_inverse, *tables]
    new, residual, coarse = pl.pallas_call(
        functools.partial(kernel, groups, members),
        out_shape=results,
        in_specs=[pl.BlockSpec(memory_space=pl.ANY)] * INPUTS,
        out_specs=[pl.BlockSpec(memory_space=pl.ANY)] * 3,
        scratch_shapes=[pltpu.VMEM(t.shape, t.dtype) for t in operands]
        + [pltpu.VMEM(t.shape, F32) for t in results]
        + [
            pltpu.VMEM((t.shape[0] * by_rows, t.shape[1] * by_columns), BF16)
            for t, by_rows, by_columns in zip(tables, (1, 3, 1, 1, 1, 1, 3, 3, 1), (1, 1, 2, 2, 1, 1, 1, 1, 1))
        ]
        + [
            pltpu.VMEM(clamp.shape, jnp.int32),
            pltpu.VMEM(coarse_owner.shape, jnp.int32),
            pltpu.VMEM((3, ny, nz), F32),
            pltpu.VMEM((3, ny, nz), F32),
            pltpu.VMEM((2, 8, vertices), F32),
            pltpu.VMEM((2 * groups, 8, vertices), F32),
            pltpu.VMEM((blocks, 1, wide), F32),
            pltpu.VMEM((2 * groups, 1, wide), F32),
            pltpu.VMEM((3 * ny + 8, nz), F32),
            pltpu.VMEM((3 * ny + 8, nz), F32),
            pltpu.VMEM((blocks, wide, wide), BF16),
            pltpu.VMEM((blocks, wide, wide), BF16),
            pltpu.VMEM((NQ, 256), F32),
            pltpu.VMEM((2 * NQ, 768), F32),
            pltpu.VMEM((NQ, 768), F32),
            pltpu.VMEM((2 * NQ, 768), F32),
            pltpu.VMEM((NQ, 768), F32),
            pltpu.VMEM((9, NQ, 256), F32),
            pltpu.VMEM((6, NQ, 256), F32),
            pltpu.VMEM((6 * NQ, 256), BF16),
            pltpu.VMEM((6 * NQ, 256), BF16),
            pltpu.VMEM((3 * NQ, 256), BF16),
            pltpu.VMEM((3 * NQ, 256), BF16),
            pltpu.SemaphoreType.DMA((4,)),
            pltpu.SemaphoreType.DMA((4,)),
            pltpu.SemaphoreType.DMA((2 * groups,)),
            pltpu.SemaphoreType.DMA((2 * groups,)),
            pltpu.SemaphoreType.DMA((2 * groups,)),
            pltpu.SemaphoreType.DMA((2 * groups,)),
            pltpu.SemaphoreType.DMA((2,)),
            pltpu.SemaphoreType.DMA((2,)),
            pltpu.SemaphoreType.DMA((INPUTS,)),
            pltpu.SemaphoreType.DMA((4,)),
        ],
        compiler_params=pltpu.CompilerParams(
            collective_id=0, has_side_effects=True, vmem_limit_bytes=56 * 1024 * 1024
        ),
    )(*operands)
    return pl.pallas_call(
        write_out,
        out_shape=results,
        in_specs=[pl.BlockSpec(memory_space=pl.ANY)] * 3,
        out_specs=[pl.BlockSpec(memory_space=pl.ANY)] * 3,
        scratch_shapes=[pltpu.VMEM(t.shape, F32) for t in results] + [pltpu.SemaphoreType.DMA((6,))],
        compiler_params=pltpu.CompilerParams(vmem_limit_bytes=56 * 1024 * 1024),
    )(new, residual, coarse)


def solution(mesh):
    in_specs = (
        P(None, ("grp", "mem"), None, None),
        P(None, ("grp", "mem"), None, None),
        P(None, ("grp", "mem"), None, None),
        P(("grp", "mem"), None),
        P(("grp", "mem"), None, None),
        P(("grp", "mem"), None),
        P(("grp", "mem"), None, None, None),
    )
    out_specs = (
        P(None, ("grp", "mem"), None, None),
        P(None, ("grp", "mem"), None, None),
        P(None, ("grp", "mem"), None, None),
    )
    body = functools.partial(shards, mesh.shape["grp"], mesh.shape["mem"])
    return jax.shard_map(body, mesh=mesh, in_specs=in_specs, out_specs=out_specs, check_vma=False)
```
